128 devices in a mesh: nodes: 32 (over z, x, core), batch: 4 (over y).
Axes of the slice: x: 4, y: 4, z: 4, core: 2. Of those that a mesh axis runs over, the one named last changes fastest.
Arguments:
- node_latents: bfloat16 [4, 8192, 512], P('batch', 'nodes'), may hold values from -6 to 6
- edge_latents: bfloat16 [4, 65536, 512], P('batch', 'nodes'), may hold values from -6 to 6
- node_cotangent: bfloat16 [4, 8192, 512], P('batch', 'nodes'), may hold values from -6 to 6
- edge_cotangent: bfloat16 [4, 65536, 512], P('batch', 'nodes'), may hold values from -6 to 6
- senders: int32 [65536], P('nodes'), may hold values from 0 to 767, as said below
- receivers: int32 [65536], P('nodes'), may hold values from 0 to 255, as said below
- send_rows: int32 [32, 32, 16], P('nodes'), may hold values from 0 to 255, as said below
- edge_weight_in: bfloat16 [1536, 512], replicated, may hold values from -0.15625 to 0.15625
- edge_bias: float32 [512], replicated, may hold values from -3 to 3
- edge_weight_out: bfloat16 [512, 512], replicated, may hold values from -0.25 to 0.25
- edge_gain: float32 [512], replicated, may hold values from 0.5 to 1.5
- node_weight_in: bfloat16 [1024, 512], replicated, may hold values from -0.1875 to 0.1875
- node_bias: float32 [512], replicated, may hold values from -3 to 3
- node_weight_out: bfloat16 [512, 512], replicated, may hold values from -0.25 to 0.25
- node_gain: float32 [512], replicated, may hold values from 0.5 to 1.5
Outputs:
- grad_nodes: bfloat16 [4, 8192, 512], P('batch', 'nodes')
- grad_edges: bfloat16 [4, 65536, 512], P('batch', 'nodes')
- grad_edge_weight_in: float32 [1536, 512], P(('nodes', 'batch'))
- grad_edge_bias: float32 [512], P(('nodes', 'batch'))
- grad_edge_weight_out: float32 [512, 512], P(('nodes', 'batch'))
- grad_edge_gain: float32 [512], P(('nodes', 'batch'))
- grad_node_weight_in: float32 [1024, 512], P(('nodes', 'batch'))
- grad_node_bias: float32 [512], P(('nodes', 'batch'))
- grad_node_weight_out: float32 [512, 512], P(('nodes', 'batch'))
- grad_node_gain: float32 [512], P(('nodes', 'batch'))
The draws below stay inside these ranges and needn't reach their ends.
Inputs may be any that keep to these rules, and one draw needn't show every extreme that they name: `senders`: values below 256 are rows of the edge's own device; a value 256 + p * 16 + s names slot s of the list that peer p holds for the edge's device, p never the edge's own device. Most remote edges name the two devices beside the owner in index order (cyclically); the rest name any device. Slots that no edge names carry padding rows. `receivers`: rows of the edge's own device. send_rows[p, d, s] is a row of device p; rows may repeat.
All inputs are finite; a program needn't handle non-finite values.
Results may differ from the reference program's by a relative error of at most 0.012.
Values may be sent and summed in bfloat16 or wider, within the bound.
No kernel may reach another device: no remote copies, remote signals or barrier semaphores. Data moves between devices by JAX's collectives and lax.ppermute only.
A program may use at most 128 MiB of HBM per device.

```python
import jax
import jax.numpy as jnp
from jax import lax

D = 512
NODE_DEV = 256
CAP = 16
EDGE_DEV = 2048
NPART = 32
NODES = 8192
EDGES = 65536
BATCH = 4


def graph_tables(key):
    keys = jax.random.split(key, 7)
    send_rows = jax.random.randint(keys[0], (NPART, NPART, CAP), 0, NODE_DEV, dtype=jnp.int32)
    send_rows = send_rows.at[0, 1, 0].set(0).at[0, 1, 1].set(NODE_DEV - 1)
    receivers = jax.random.randint(keys[1], (EDGES,), 0, NODE_DEV, dtype=jnp.int32)
    receivers = receivers.at[0].set(0).at[1].set(NODE_DEV - 1)
    owner_part = jnp.arange(EDGES, dtype=jnp.int32) // EDGE_DEV
    position = jnp.arange(EDGES, dtype=jnp.int32) % EDGE_DEV
    kind_draw = jax.random.randint(keys[2], (EDGES,), 0, 8, dtype=jnp.int32)
    local_rows = jax.random.randint(keys[3], (EDGES,), 0, NODE_DEV, dtype=jnp.int32)
    side_draw = jax.random.randint(keys[4], (EDGES,), 0, 2, dtype=jnp.int32)
    near_offset = jnp.where(side_draw == 0, 1, NPART - 1)
    far_offset = jax.random.randint(keys[5], (EDGES,), 1, NPART, dtype=jnp.int32)
    offset = jnp.where(kind_draw == 7, far_offset, near_offset)
    peer_part = (owner_part + offset) % NPART
    slot_draw = jax.random.randint(keys[6], (EDGES,), 0, CAP, dtype=jnp.int32)
    remote_refs = NODE_DEV + peer_part * CAP + slot_draw
    senders = jnp.where(kind_draw < 4, local_rows, remote_refs)
    corner_ref = NODE_DEV + (owner_part + NPART - 1) % NPART * CAP + CAP - 1
    senders = jnp.where(position == EDGE_DEV - 1, corner_ref, senders)
    senders = jnp.where(position == EDGE_DEV - 2, 0, senders)
    return (senders.astype(jnp.int32), receivers, send_rows)


def draw_senders(key, part):
    return graph_tables(key)[0]


def draw_receivers(key, part):
    return graph_tables(key)[1]


def draw_send_rows(key, part):
    return graph_tables(key)[2]


def steps_of(own_key, dims, cuts, smallest, top_value):
    level = 1.0
    for dim, shards_of in cuts:
        heights = jax.random.uniform(jax.random.fold_in(jax.random.fold_in(own_key, 6), dim), (shards_of,), jnp.float32, smallest / len(cuts), top_value / len(cuts))
        level = level * jnp.repeat(jnp.exp(heights), dims[dim] // shards_of).reshape((-1,) + (1,) * (len(dims) - 1 - dim))
    return level


def noise(rng, extent, deviation, bound, pieces=(), kind=jnp.bfloat16):
    level = steps_of(rng, extent, pieces, -0.22, 0.18) if pieces else 1.0
    entries = jax.random.normal(rng, extent, jnp.float32) * deviation * level
    return jnp.minimum(jnp.maximum(entries, -bound), bound).astype(kind)


def setup_inputs(seed: int = 0) -> dict:
    key_list = jax.random.split(jax.random.key(seed), 16)
    return {
        "node_latents": noise(key_list[0], (BATCH, NODES, D), 1.0, 6.0, ((0, 4), (1, 32))),
        "edge_latents": noise(key_list[1], (BATCH, EDGES, D), 1.0, 6.0, ((0, 4), (1, 32))),
        "node_cotangent": noise(key_list[2], (BATCH, NODES, D), 1.0, 6.0, ((0, 4), (1, 32))),
        "edge_cotangent": noise(key_list[3], (BATCH, EDGES, D), 1.0, 6.0, ((0, 4), (1, 32))),
        "senders": draw_senders(jax.random.fold_in(key_list[15], 71), 0),
        "receivers": draw_receivers(jax.random.fold_in(key_list[15], 71), 0),
        "send_rows": draw_send_rows(jax.random.fold_in(key_list[15], 71), 0),
        "edge_weight_in": noise(key_list[7], (3 * D, D), (3 * D) ** -0.5, 0.15625),
        "edge_bias": noise(key_list[8], (D,), 0.5, 3.0, (), jnp.float32),
        "edge_weight_out": noise(key_list[9], (D, D), D ** -0.5, 0.25),
        "edge_gain": jnp.clip(1.0 + 0.1 * jax.random.normal(key_list[10], (D,), jnp.float32), 0.5, 1.5),
        "node_weight_in": noise(key_list[11], (2 * D, D), (2 * D) ** -0.5, 0.1875),
        "node_bias": noise(key_list[12], (D,), 0.5, 3.0, (), jnp.float32),
        "node_weight_out": noise(key_list[13], (D, D), D ** -0.5, 0.25),
        "node_gain": jnp.clip(1.0 + 0.1 * jax.random.normal(key_list[14], (D,), jnp.float32), 0.5, 1.5),
    }


EPS = 1e-05

def silu_slope(values):
    sigmoid_v = jax.nn.sigmoid(values)
    return sigmoid_v * (1.0 + values * (1.0 - sigmoid_v))

def mlp_forward(layer_input, weight_in, bias_vec, weight_out):
    pre_act = jnp.dot(layer_input, weight_in, preferred_element_type=jnp.float32) + bias_vec
    activation = jax.nn.silu(pre_act).astype(jnp.bfloat16)
    pre_norm = jnp.dot(activation, weight_out, preferred_element_type=jnp.float32)
    row_mean = lax.optimization_barrier(jnp.mean(pre_norm, axis=-1, keepdims=True))
    centred = pre_norm - row_mean
    inv_scale = lax.rsqrt(lax.optimization_barrier(jnp.mean(centred * centred, axis=-1, keepdims=True)) + EPS)
    return (pre_act, activation, centred * inv_scale, inv_scale)

def mlp_backward(layer_input, pre_act, activation, normed, inv_scale, weight_in, weight_out, gain_vec, grad_out):
    dims_rows = (((0,), (0,)), ((), ()))
    dims_cols = (((1,), (1,)), ((), ()))
    grad_gain = lax.optimization_barrier(jnp.sum(grad_out * normed, axis=0))
    scaled = grad_out * gain_vec
    grad_norm = ((scaled - lax.optimization_barrier(jnp.mean(scaled, axis=-1, keepdims=True)) - normed * lax.optimization_barrier(jnp.mean(scaled * normed, axis=-1, keepdims=True))) * inv_scale).astype(jnp.bfloat16)
    grad_second = lax.dot_general(activation, grad_norm, dims_rows, preferred_element_type=jnp.float32)
    grad_act = lax.dot_general(grad_norm, weight_out, dims_cols, preferred_element_type=jnp.float32)
    grad_pre = (grad_act * silu_slope(pre_act)).astype(jnp.bfloat16)
    grad_bias = lax.optimization_barrier(jnp.sum(grad_pre.astype(jnp.float32), axis=0))
    grad_first = lax.dot_general(layer_input, grad_pre, dims_rows, preferred_element_type=jnp.float32)
    grad_input = lax.dot_general(grad_pre, weight_in, dims_cols, preferred_element_type=jnp.float32)
    return (grad_input, grad_first, grad_bias, grad_second, grad_gain)

def reference(node_latents, edge_latents, node_cotangent, edge_cotangent, senders, receivers, send_rows, edge_weight_in, edge_bias, edge_weight_out, edge_gain, node_weight_in, node_bias, node_weight_out, node_gain):
    owner_part = jnp.arange(EDGES, dtype=jnp.int32) // EDGE_DEV
    receiver_node = owner_part * NODE_DEV + receivers
    halo_slot = jnp.maximum(senders - NODE_DEV, 0)
    peer_part = halo_slot // CAP
    listed = send_rows[peer_part, owner_part, halo_slot % CAP]
    sender_node = jnp.where(senders >= NODE_DEV, peer_part * NODE_DEV + listed, owner_part * NODE_DEV + senders)

    def one_state(state):
        node_rows, edge_rows, node_cot, edge_cot = state
        edge_input = jnp.concatenate([edge_rows, node_rows[sender_node], node_rows[receiver_node]], axis=1)
        edge_pre, edge_act, edge_norm, edge_inv = mlp_forward(edge_input, edge_weight_in, edge_bias, edge_weight_out)
        message = (edge_norm * edge_gain).astype(jnp.bfloat16)
        aggregate = jax.ops.segment_sum(message.astype(jnp.float32), receiver_node, NODES).astype(jnp.bfloat16)
        node_input = jnp.concatenate([node_rows, aggregate], axis=1)
        node_pre, node_act, node_norm, node_inv = mlp_forward(node_input, node_weight_in, node_bias, node_weight_out)
        node_grads = mlp_backward(node_input, node_pre, node_act, node_norm, node_inv, node_weight_in, node_weight_out, node_gain, node_cot.astype(jnp.float32))
        node_grad_input = node_grads[0]
        message_grad = edge_cot.astype(jnp.float32) + node_grad_input[:, D:][receiver_node]
        edge_grads = mlp_backward(edge_input, edge_pre, edge_act, edge_norm, edge_inv, edge_weight_in, edge_weight_out, edge_gain, message_grad)
        edge_grad_input = edge_grads[0]
        grad_edges = (edge_cot.astype(jnp.float32) + edge_grad_input[:, :D]).astype(jnp.bfloat16)
        grad_nodes = (node_cot.astype(jnp.float32) + node_grad_input[:, :D] + jax.ops.segment_sum(edge_grad_input[:, 2 * D:], receiver_node, NODES) + jax.ops.segment_sum(edge_grad_input[:, D:2 * D], sender_node, NODES)).astype(jnp.bfloat16)
        return (grad_nodes, grad_edges) + tuple(edge_grads[1:]) + tuple(node_grads[1:])
    results = lax.map(one_state, (node_latents, edge_latents, node_cotangent, edge_cotangent))
    factor = 1.0 / (BATCH * EDGES) ** 0.5
    summed = [lax.optimization_barrier(jnp.sum(item, axis=0)) * factor for item in results[2:]]
    return (results[0], results[1], summed[0], summed[1], summed[2], summed[3], summed[4], summed[5], summed[6], summed[7])
```

```python
import functools
import math

import jax
import jax.numpy as jnp
from jax import lax
from jax.experimental import pallas as pl
from jax.experimental.pallas import tpu as pltpu
from jax.sharding import PartitionSpec as P

EPS = 1e-05
ALL = ("nodes", "batch")
F32 = jnp.float32
BF16 = jnp.bfloat16
TILE = 512
LANES = 128
EDGE_IN, EDGE_OUT, NODE_IN, NODE_OUT = 48, 16, 32, 16
HALO = 16
EDGE_ROWS = HALO + EDGE_IN + EDGE_OUT
NODE_ROWS = NODE_IN + NODE_OUT
SENT_ROWS = 2 * HALO + EDGE_IN + EDGE_OUT + NODE_ROWS
SMALL = 16
VMEM_LIMIT = 48 * 1024 * 1024


def nn(lhs, rhs):
    return lax.dot_general(lhs, rhs, (((1,), (0,)), ((), ())), preferred_element_type=F32)


def nt(lhs, rhs):
    return lax.dot_general(lhs, rhs, (((1,), (1,)), ((), ())), preferred_element_type=F32)


def tn(lhs, rhs):
    return lax.dot_general(lhs, rhs, (((0,), (0,)), ((), ())), preferred_element_type=F32)


def pick_rows(index_column, count, first=0):
    shape = (index_column.shape[0], count)
    columns = lax.broadcasted_iota(jnp.int32, shape, 1) + first
    return jnp.where(index_column == columns, 1.0, 0.0).astype(BF16)


def pick_columns(index_row, count, first=0):
    shape = (count, index_row.shape[1])
    rows = lax.broadcasted_iota(jnp.int32, shape, 0) + first
    return jnp.where(index_row == rows, 1.0, 0.0).astype(BF16)


def activate(pre):
    sig = jax.nn.sigmoid(pre)
    return pre * sig, sig * (1.0 + pre * (1.0 - sig))


def layer_norm(pre_norm):
    centred = pre_norm - jnp.mean(pre_norm, axis=-1, keepdims=True)
    inv = lax.rsqrt(jnp.mean(centred * centred, axis=-1, keepdims=True) + EPS)
    return centred * inv, inv


def norm_backward(scaled, normed, inv):
    mean_scaled = jnp.mean(scaled, axis=-1, keepdims=True)
    mean_product = jnp.mean(scaled * normed, axis=-1, keepdims=True)
    return (scaled - mean_scaled - normed * mean_product) * inv


def put(dst, chip, stride, row, block):
    count = block.shape[0]
    for group in range(4):
        dst[chip, pl.ds(group * stride + row, count), :] = block[
            :, group * LANES : (group + 1) * LANES
        ].astype(BF16)


def gather_kernel(rows_ref, hidden_ref, out_ref):
    out_ref[...] = nn(pick_rows(rows_ref[...], hidden_ref.shape[0]), hidden_ref[...]).astype(BF16)


def local_kernel(
    edge_ref, index_ref, hidden_ref, weight_ref, bias_ref, nweight_ref, nbias_ref,
    part_ref, npart_ref, table
):
    width = hidden_ref.shape[1]
    nodes = hidden_ref.shape[0]

    @pl.when(pl.program_id(0) == 0)
    def _():
        hidden = hidden_ref[...]
        table[:nodes] = nn(hidden, weight_ref[width : 2 * width]).astype(BF16)
        table[nodes:] = nn(hidden, weight_ref[2 * width :]).astype(BF16)
        npart_ref[...] = nn(hidden, nweight_ref[...]) + nbias_ref[...]

    index = index_ref[...]
    picks = jnp.concatenate(
        [pick_rows(index[:, 0:1], nodes), pick_rows(index[:, 1:2], nodes)], axis=1
    )
    part_ref[...] = (
        nn(edge_ref[...], weight_ref[:width]) + nn(picks, table[...]) + bias_ref[...]
    )


def forward_kernel(
    core_ref, part_ref, index_ref, rows_ref, halo_ref, weight_ref, weight_out_ref, gain_ref,
    hidden_ref, npart_ref, nweight_ref, nweight_out_ref, ngain_ref, ncot_ref,
    act_ref, slope_ref, norm_ref, inv_ref, base_ref, agg_grad_ref, nsend_ref, nkeep_ref,
    nsmall_ref, table, aggregate, grad_in, grad_out
):
    step = pl.program_id(0)
    nodes, width = hidden_ref.shape
    slots = halo_ref.shape[0]

    @pl.when(step == 0)
    def _():
        table[...] = nn(halo_ref[...], weight_ref[...]).astype(BF16)
        aggregate[...] = jnp.zeros_like(aggregate)

    pre = part_ref[...] + nn(pick_rows(index_ref[:, 0:1], slots, nodes), table[...])
    act, slope = activate(pre)
    act = act.astype(BF16)
    act_ref[...] = act
    slope_ref[...] = slope.astype(BF16)
    normed, inv = layer_norm(nn(act, weight_out_ref[...]))
    norm_ref[...] = normed.astype(BF16)
    inv_ref[...] = inv
    message = (normed * gain_ref[...]).astype(BF16)
    aggregate[...] += nn(pick_columns(rows_ref[1:2, :], nodes), message)

    @pl.when(step == pl.num_programs(0) - 1)
    def _():
        hidden = hidden_ref[...]
        received = aggregate[...].astype(BF16)
        node_act, node_slope = activate(npart_ref[...] + nn(received, nweight_ref[width:]))
        node_act = node_act.astype(BF16)
        node_norm, node_inv = layer_norm(nn(node_act, nweight_out_ref[...]))
        cot = ncot_ref[...].astype(F32)
        nsmall_ref[1:2] = jnp.sum(cot * node_norm, axis=0, keepdims=True)
        grad_norm = norm_backward(cot * ngain_ref[...], node_norm, node_inv).astype(BF16)
        grad_pre = (nt(grad_norm, nweight_out_ref[...]) * node_slope).astype(BF16)
        nsmall_ref[0:1] = jnp.sum(grad_pre.astype(F32), axis=0, keepdims=True)
        agg_grad_ref[...] = nt(grad_pre, nweight_ref[width:]).astype(BF16)
        base_ref[...] = cot + nt(grad_pre, nweight_ref[:width])
        grad_out[...] = tn(node_act, grad_norm)
        grad_in[:width] = tn(hidden, grad_pre)
        grad_in[width:] = tn(received, grad_pre)
        core = core_ref[0]
        for dst, side in ((nkeep_ref, core), (nsend_ref, 1 - core)):

            def pack(chip, carry):
                piece = chip * 2 + side
                start = pl.multiple_of(piece * NODE_IN, NODE_IN)
                put(dst, chip, NODE_ROWS, 0, grad_in[pl.ds(start, NODE_IN)])
                start = pl.multiple_of(piece * NODE_OUT, NODE_OUT)
                put(dst, chip, NODE_ROWS, NODE_IN, grad_out[pl.ds(start, NODE_OUT)])
                return carry

            lax.fori_loop(0, dst.shape[0], pack, 0)


def backward_kernel(
    core_ref, ecot_ref, index_ref, rows_ref, act_ref, slope_ref, norm_ref, inv_ref, edge_ref,
    agg_grad_ref, gain_ref, weight_out_ref, weight_ref, hidden_ref, halo_ref, base_ref, nsmall_ref,
    pre_grad_ref, esend_ref, ekeep_ref, total_ref,
    grad_in, grad_out, sums, terms, bias_sum, gain_sum
):
    step = pl.program_id(0)
    nodes, width = hidden_ref.shape
    slots = halo_ref.shape[0]

    @pl.when(step == 0)
    def _():
        grad_in[...] = jnp.zeros_like(grad_in)
        grad_out[...] = jnp.zeros_like(grad_out)
        sums[...] = jnp.zeros_like(sums)
        bias_sum[...] = jnp.zeros_like(bias_sum)
        gain_sum[...] = jnp.zeros_like(gain_sum)

    message_grad = ecot_ref[...].astype(F32) + nn(
        pick_rows(index_ref[:, 1:2], nodes), agg_grad_ref[...]
    )
    normed = norm_ref[...].astype(F32)
    gain_sum[...] += jnp.sum(message_grad * normed, axis=0, keepdims=True)
    grad_norm = norm_backward(message_grad * gain_ref[...], normed, inv_ref[...]).astype(BF16)
    grad_pre = nt(grad_norm, weight_out_ref[...]) * slope_ref[...].astype(F32)
    grad_pre = grad_pre.astype(BF16)
    pre_grad_ref[...] = grad_pre
    bias_sum[...] += jnp.sum(grad_pre.astype(F32), axis=0, keepdims=True)
    grad_out[...] += tn(act_ref[...], grad_norm)
    grad_in[:width] += tn(edge_ref[...], grad_pre)
    sums[: nodes + slots] += nn(pick_columns(rows_ref[0:1, :], nodes + slots), grad_pre)
    sums[nodes + slots :] += nn(pick_columns(rows_ref[1:2, :], nodes), grad_pre)

    @pl.when(step == pl.num_programs(0) - 1)
    def _():
        own = sums[:nodes].astype(BF16)
        remote = sums[nodes : nodes + slots].astype(BF16)
        received = sums[nodes + slots :].astype(BF16)
        hidden = hidden_ref[...]
        grad_in[width : 2 * width] = tn(hidden, own) + tn(halo_ref[...], remote)
        grad_in[2 * width :] = tn(hidden, received)
        terms[...] = nt(remote, weight_ref[width : 2 * width])
        total_ref[...] = (
            base_ref[...]
            + nt(own, weight_ref[width : 2 * width])
            + nt(received, weight_ref[2 * width :])
        )
        small = [bias_sum[...], gain_sum[...], nsmall_ref[0:1], nsmall_ref[1:2]]
        small = jnp.concatenate(
            [item[:, g * LANES : (g + 1) * LANES] for item in small for g in range(4)], axis=0
        ).astype(BF16)
        core = core_ref[0]
        for dst, side in ((ekeep_ref, core), (esend_ref, 1 - core)):

            def pack(chip, carry):
                piece = chip * 2 + side
                start = pl.multiple_of(piece * HALO, HALO)
                put(dst, chip, EDGE_ROWS, 0, terms[pl.ds(start, HALO)])
                start = pl.multiple_of(piece * EDGE_IN, EDGE_IN)
                put(dst, chip, EDGE_ROWS, HALO, grad_in[pl.ds(start, EDGE_IN)])
                start = pl.multiple_of(piece * EDGE_OUT, EDGE_OUT)
                put(dst, chip, EDGE_ROWS, HALO + EDGE_IN, grad_out[pl.ds(start, EDGE_OUT)])
                dst[chip, 4 * EDGE_ROWS :, :] = small
                return carry

            lax.fori_loop(0, dst.shape[0], pack, 0)


def pair_kernel(core_ref, ekeep_ref, erecv_ref, nkeep_ref, nrecv_ref, out_ref):
    core = core_ref[0]

    def add(lhs, rhs, start, count):
        rows = slice(start, start + count)
        return (lhs[:, rows, :].astype(F32) + rhs[:, rows, :].astype(F32)).astype(BF16)

    for group in range(4):
        out, edge, node = group * SENT_ROWS, group * EDGE_ROWS, group * NODE_ROWS
        start = pl.multiple_of(out + core * HALO, HALO)
        out_ref[:, pl.ds(start, HALO), :] = ekeep_ref[:, edge : edge + HALO, :]
        start = pl.multiple_of(out + (1 - core) * HALO, HALO)
        out_ref[:, pl.ds(start, HALO), :] = erecv_ref[:, edge : edge + HALO, :]
        out += 2 * HALO
        count = EDGE_IN + EDGE_OUT
        out_ref[:, out : out + count, :] = add(ekeep_ref, erecv_ref, edge + HALO, count)
        out += count
        out_ref[:, out : out + NODE_ROWS, :] = add(nkeep_ref, nrecv_ref, node, NODE_ROWS)
    out_ref[:, 4 * SENT_ROWS :, :] = add(ekeep_ref, erecv_ref, 4 * EDGE_ROWS, SMALL)


def edge_out_kernel(ecot_ref, pre_grad_ref, weight_ref, out_ref):
    out_ref[...] = (
        ecot_ref[...].astype(F32) + nt(pre_grad_ref[...], weight_ref[...])
    ).astype(BF16)


def arrive_kernel(
    batch_ref, arrived_ref, rows_ref, total_ref, nodes_ref, mine_ref, one_ref, two_ref, three_ref, sums
):
    nodes = total_ref.shape[0]
    picks = pick_columns(rows_ref[...], nodes)
    for group in range(4):
        out = group * SENT_ROWS
        halo = arrived_ref[:, out : out + 2 * HALO, :].reshape(-1, LANES)
        lanes = slice(group * LANES, (group + 1) * LANES)
        nodes_ref[:, lanes] = (total_ref[:, lanes] + nn(picks, halo)).astype(BF16)
        weights = jnp.sum(
            arrived_ref[:, out + 2 * HALO : out + SENT_ROWS, :].astype(F32), axis=0
        )
        for state in range(4):
            row, first = group * 28, 0
            for count in (EDGE_IN, EDGE_OUT, NODE_IN, NODE_OUT):
                share = count // 4
                begin = first + state * share
                sums[state, row : row + share, :] = weights[begin : begin + share, :]
                row += share
                first += count
    small = jnp.sum(arrived_ref[:, 4 * SENT_ROWS :, :].astype(F32), axis=0)
    for state in range(4):
        sums[state, 112:, :] = small
    batch = batch_ref[0]
    mine_ref[...] = sums[batch]
    for away, ref in ((1, one_ref), (2, two_ref), (3, three_ref)):
        ref[...] = sums[lax.rem(batch + away, 4)].astype(BF16)


def finish_kernel(
    factor, mine_ref, one_ref, two_ref, three_ref,
    edge_in_ref, edge_out_ref, node_in_ref, node_out_ref, small_ref
):
    total = (
        mine_ref[...]
        + one_ref[...].astype(F32)
        + two_ref[...].astype(F32)
        + three_ref[...].astype(F32)
    ) * factor
    for group in range(4):
        lanes = slice(group * LANES, (group + 1) * LANES)
        row = group * 28
        for ref in (edge_in_ref, edge_out_ref, node_in_ref, node_out_ref):
            count = ref.shape[0]
            ref[:, lanes] = total[row : row + count, :]
            row += count
    small_ref[...] = total[112:, :]


def call(body, outs, grid=None, in_specs=None, out_specs=None, scratch=(), cost=None):
    args = {}
    if grid is not None:
        args = dict(grid=grid, in_specs=in_specs, out_specs=out_specs)
    elif in_specs is not None:
        args = dict(in_specs=in_specs)
    return pl.pallas_call(
        body,
        out_shape=outs,
        scratch_shapes=scratch,
        compiler_params=pltpu.CompilerParams(vmem_limit_bytes=VMEM_LIMIT),
        cost_estimate=cost,
        **args,
    )


def flops(count, moved):
    return pl.CostEstimate(flops=int(count), bytes_accessed=int(moved), transcendentals=0)


def shape(*dims, dtype=BF16):
    return jax.ShapeDtypeStruct(dims, dtype)


def full(*dims):
    return pl.BlockSpec(dims, lambda i: (0,) * len(dims))


def tiled(*dims):
    return pl.BlockSpec(dims, lambda i: (i,) + (0,) * (len(dims) - 1))


SCALAR = pl.BlockSpec(memory_space=pltpu.SMEM)
WHOLE = pl.BlockSpec(memory_space=pltpu.VMEM)


def shards(
    node_latents, edge_latents, node_cotangent, edge_cotangent, senders, receivers, send_rows,
    edge_weight_in, edge_bias, edge_weight_out, edge_gain,
    node_weight_in, node_bias, node_weight_out, node_gain,
):
    nodes, width = node_latents.shape[1:]
    edges = edge_latents.shape[1]
    parts = lax.axis_size("nodes")
    batch_size = lax.axis_size("batch")
    slots = send_rows.shape[1] * send_rows.shape[2]
    chips = parts // 2
    hidden = node_latents[0]
    edge_rows = edge_latents[0]
    ncot = node_cotangent[0]
    ecot = edge_cotangent[0]
    node_index = lax.axis_index("nodes")
    core = jnp.reshape(node_index % 2, (1,)).astype(jnp.int32)
    batch = jnp.reshape(lax.axis_index("batch"), (1,)).astype(jnp.int32)
    tile = min(TILE, edges)
    grid = (edges // tile,)

    row = lambda vector: vector.reshape(1, width)
    index = jnp.stack([senders, receivers], axis=1)
    index_rows = jnp.stack([senders, receivers], axis=0)

    with jax.named_scope("halo_rows"):
        outgoing = call(gather_kernel, shape(slots, width))(send_rows.reshape(slots, 1), hidden)
        halo = lax.all_to_all(
            outgoing.reshape(parts, -1, width), "nodes", 0, 0, tiled=True
        ).reshape(slots, width)
    index_tile = tiled(tile, 2)
    rows_tile = pl.BlockSpec((2, tile), lambda i: (0, i))
    edge_tile = tiled(tile, width)
    with jax.named_scope("edge_pre_local"):
        part, npart = call(
            local_kernel,
            (shape(edges, width, dtype=F32), shape(nodes, width, dtype=F32)),
            grid,
            [
                edge_tile, index_tile, full(nodes, width), full(3 * width, width), full(1, width),
                full(width, width), full(1, width),
            ],
            (edge_tile, full(nodes, width)),
            [pltpu.VMEM((2 * nodes, width), BF16)],
            flops(2 * edges * width * 2 * width, 6 * edges * width),
        )(edge_rows, index, hidden, edge_weight_in, row(edge_bias), node_weight_in, row(node_bias))
    with jax.named_scope("forward"):
        node_pack = shape(chips, 4 * NODE_ROWS, LANES)
        act, slope, norm, inv, base, agg_grad, nsend, nkeep, nsmall = call(
            forward_kernel,
            (
                shape(edges, width), shape(edges, width), shape(edges, width),
                shape(edges, 1, dtype=F32), shape(nodes, width, dtype=F32), shape(nodes, width),
                node_pack, node_pack, shape(2, width, dtype=F32),
            ),
            grid,
            [
                SCALAR, edge_tile, index_tile, rows_tile, full(slots, width),
                pl.BlockSpec((width, width), lambda i: (1, 0)), full(width, width), full(1, width),
                full(nodes, width), full(nodes, width), full(2 * width, width), full(width, width),
                full(1, width), full(nodes, width),
            ],
            (
                edge_tile, edge_tile, edge_tile, tiled(tile, 1), full(nodes, width),
                full(nodes, width), full(*node_pack.shape), full(*node_pack.shape), full(2, width),
            ),
            [
                pltpu.VMEM((slots, width), BF16), pltpu.VMEM((nodes, width), F32),
                pltpu.VMEM((2 * width, width), F32), pltpu.VMEM((width, width), F32),
            ],
            flops(2 * edges * width * 3 * width, 12 * edges * width),
        )(
            core, part, index, index_rows, halo, edge_weight_in, edge_weight_out, row(edge_gain),
            hidden, npart, node_weight_in, node_weight_out, row(node_gain), ncot,
        )
    partner = [(i, i ^ batch_size) for i in range(parts * batch_size)]
    with jax.named_scope("node_weight_pair"):
        nrecv = lax.ppermute(nsend, ALL, partner)
    with jax.named_scope("backward"):
        edge_pack = shape(chips, 4 * EDGE_ROWS + SMALL, LANES)
        pre_grad, esend, ekeep, total = call(
            backward_kernel,
            (shape(edges, width), edge_pack, edge_pack, shape(nodes, width, dtype=F32)),
            grid,
            [
                SCALAR, edge_tile, index_tile, rows_tile, edge_tile, edge_tile, edge_tile,
                tiled(tile, 1), edge_tile, full(nodes, width), full(1, width), full(width, width),
                full(3 * width, width), full(nodes, width), full(slots, width), full(nodes, width),
                full(2, width),
            ],
            (edge_tile, full(*edge_pack.shape), full(*edge_pack.shape), full(nodes, width)),
            [
                pltpu.VMEM((3 * width, width), F32), pltpu.VMEM((width, width), F32),
                pltpu.VMEM((2 * nodes + slots, width), F32), pltpu.VMEM((slots, width), F32),
                pltpu.VMEM((1, width), F32), pltpu.VMEM((1, width), F32),
            ],
            flops(2 * edges * width * 6 * width, 14 * edges * width),
        )(
            core, ecot, index, index_rows, act, slope, norm, inv, edge_rows, agg_grad,
            row(edge_gain), edge_weight_out, edge_weight_in, hidden, halo, base, nsmall,
        )
    with jax.named_scope("edge_weight_pair"):
        erecv = lax.ppermute(esend, ALL, partner)
    with jax.named_scope("pair_sum"):
        sent = call(
            pair_kernel,
            shape(chips, 4 * SENT_ROWS + SMALL, LANES),
            (4,),
            [
                SCALAR, tiled(chips // 4, *edge_pack.shape[1:]), tiled(chips // 4, *edge_pack.shape[1:]),
                tiled(chips // 4, *node_pack.shape[1:]), tiled(chips // 4, *node_pack.shape[1:]),
            ],
            tiled(chips // 4, 4 * SENT_ROWS + SMALL, LANES),
            cost=flops(0, 3 * chips * 4 * SENT_ROWS * LANES),
        )(core, ekeep, erecv, nkeep, nrecv)
    with jax.named_scope("chip_exchange"):
        groups = [[2 * chip + side for chip in range(chips)] for side in range(2)]
        arrived = lax.all_to_all(sent, "nodes", 0, 0, tiled=True, axis_index_groups=groups)
    with jax.named_scope("grad_edges"):
        grad_edges = call(
            edge_out_kernel,
            shape(edges, width),
            grid,
            [edge_tile, edge_tile, full(width, width)],
            edge_tile,
            cost=flops(2 * edges * width * width, 6 * edges * width),
        )(ecot, pre_grad, edge_weight_in)
    with jax.named_scope("arrive"):
        block = (112 + SMALL, LANES)
        grad_nodes, mine, one, two, three = call(
            arrive_kernel,
            (shape(nodes, width), shape(*block, dtype=F32), shape(*block), shape(*block), shape(*block)),
            in_specs=[SCALAR, WHOLE, WHOLE, WHOLE],
            scratch=[pltpu.VMEM((4, *block), F32)],
        )(batch, arrived, send_rows.reshape(1, slots), total)
    with jax.named_scope("state_exchange"):
        places = [
            [(n * batch_size + b, n * batch_size + (b + away) % batch_size)
             for n in range(parts) for b in range(batch_size)]
            for away in (1, 2, 3)
        ]
        got = [lax.ppermute(item, ALL, perm) for item, perm in zip((one, two, three), places)]
    with jax.named_scope("weight_grads"):
        factor = 1.0 / math.sqrt(batch_size * edges * parts)
        edge_in, edge_out, node_in, node_out, small = call(
            functools.partial(finish_kernel, factor),
            (
                shape(12, width, dtype=F32), shape(4, width, dtype=F32), shape(8, width, dtype=F32),
                shape(4, width, dtype=F32), shape(SMALL, LANES, dtype=F32),
            ),
        )(mine, *got)
        place = node_index * batch_size + lax.axis_index("batch")
        small = lax.dynamic_slice(
            small.reshape(4, width), (0, place * 4), (4, 4)
        )
    return (
        grad_nodes[None], grad_edges[None], edge_in, small[0], edge_out, small[1],
        node_in, small[2], node_out, small[3],
    )


def solution(mesh):
    rows = P("batch", "nodes", None)
    split = P(ALL, None)
    return jax.shard_map(
        shards,
        mesh=mesh,
        in_specs=(rows,) * 4 + (P("nodes"), P("nodes"), P("nodes", None, None)) + (P(),) * 8,
        out_specs=(rows, rows) + (split, P(ALL)) * 4,
        check_vma=False,
    )
```

```python
import functools
import math

import jax
import jax.numpy as jnp
from jax import lax
from jax.experimental import pallas as pl
from jax.experimental.pallas import tpu as pltpu
from jax.sharding import PartitionSpec as P

EPS = 1e-05
ALL = ("nodes", "batch")
F32 = jnp.float32
BF16 = jnp.bfloat16
TILE = 512
EDGE_IN, EDGE_OUT = 48, 16
SHARE_EDGE_IN, SHARE_EDGE_OUT, SHARE_NODE_IN, SHARE_NODE_OUT = 12, 4, 8, 4
EDGE_BLOCK = EDGE_IN + EDGE_OUT
SHARE_EDGE = SHARE_EDGE_IN + SHARE_EDGE_OUT
SHARE_NODE = 192
SHARE_ROWS = 16 * SHARE_EDGE + SHARE_NODE
SMALL = 16
STATES = 4
VMEM_FEW = 24 * 1024 * 1024
VMEM_MOST = 62 * 1024 * 1024


def nn(lhs, rhs):
    return lax.dot_general(lhs, rhs, (((1,), (0,)), ((), ())), preferred_element_type=F32)


def nt(lhs, rhs):
    return lax.dot_general(lhs, rhs, (((1,), (1,)), ((), ())), preferred_element_type=F32)


def tn(lhs, rhs):
    return lax.dot_general(lhs, rhs, (((0,), (0,)), ((), ())), preferred_element_type=F32)


def pick_rows(index_column, count, first=0):
    shape = (index_column.shape[0], count)
    columns = lax.broadcasted_iota(jnp.int32, shape, 1) + first
    return jnp.where(index_column == columns, 1.0, 0.0).astype(BF16)


def pick_columns(index_row, count, first=0):
    shape = (count, index_row.shape[1])
    rows = lax.broadcasted_iota(jnp.int32, shape, 0) + first
    return jnp.where(index_row == rows, 1.0, 0.0).astype(BF16)


def activate(pre):
    sig = jax.nn.sigmoid(pre)
    return pre * sig, sig * (1.0 + pre * (1.0 - sig))


def layer_norm(pre_norm):
    centred = pre_norm - jnp.mean(pre_norm, axis=-1, keepdims=True)
    inv = lax.rsqrt(jnp.mean(centred * centred, axis=-1, keepdims=True) + EPS)
    return centred * inv, inv


def norm_backward(scaled, normed, inv):
    mean_scaled = jnp.mean(scaled, axis=-1, keepdims=True)
    mean_product = jnp.mean(scaled * normed, axis=-1, keepdims=True)
    return (scaled - mean_scaled - normed * mean_product) * inv


def permutation(count, shares, rows):
    source = lax.broadcasted_iota(jnp.int32, (count, count), 0)
    place = lax.broadcasted_iota(jnp.int32, (count, count), 1)
    row = place % rows
    chip = (place // rows) % shares
    core = (place // (rows * shares)) % 2
    state = place // (rows * shares * 2)
    wanted = ((chip * 2 + core) * STATES + state) * rows + row
    return jnp.where(source == wanted, 1.0, 0.0).astype(BF16)


def gather_kernel(rows_ref, hidden_ref, out_ref):
    slots, peers = rows_ref.shape
    lists = rows_ref[...].astype(F32).astype(BF16)
    place = lax.broadcasted_iota(jnp.int32, (peers * slots, slots), 0)
    slot = lax.broadcasted_iota(jnp.int32, (peers * slots, slots), 1)
    spread = nn(jnp.where(place % slots == slot, 1.0, 0.0).astype(BF16), lists)
    place = lax.broadcasted_iota(jnp.int32, (peers * slots, peers), 0)
    peer = lax.broadcasted_iota(jnp.int32, (peers * slots, peers), 1)
    column = jnp.sum(
        jnp.where(place // slots == peer, spread, 0.0), axis=1, keepdims=True
    ).astype(jnp.int32)
    out_ref[...] = nn(pick_rows(column, hidden_ref.shape[0]), hidden_ref[...]).astype(BF16)


def local_kernel(
    edge_ref, rows_ref, hidden_ref, weight_ref, bias_ref, nweight_ref, nbias_ref,
    part_ref, npart_ref, ordered_ref, table
):
    width = hidden_ref.shape[1]
    nodes = hidden_ref.shape[0]

    @pl.when(pl.program_id(0) == 0)
    def _():
        hidden = hidden_ref[...]
        table[:nodes] = nn(hidden, weight_ref[width : 2 * width]).astype(BF16)
        table[nodes:] = nn(hidden, weight_ref[2 * width :]).astype(BF16)
        npart_ref[...] = nn(hidden, nweight_ref[...]) + nbias_ref[...]
        ordered_ref[...] = nn(hidden, permutation(width, 8, SHARE_NODE_IN)).astype(BF16)

    picks = jnp.concatenate(
        [pick_columns(rows_ref[0:1, :], nodes), pick_columns(rows_ref[1:2, :], nodes)], axis=0
    )
    part_ref[...] = (
        nn(edge_ref[...], weight_ref[:width]) + tn(picks, table[...]) + bias_ref[...]
    )


def forward_kernel(
    core_ref, rows_ref, gain_ref, ngain_ref, part_hbm, halo_hbm, weight_hbm, weight_out_hbm,
    ordered_hbm, npart_hbm, nweight_hbm, nweight_out_hbm, ncot_hbm,
    act_ref, slope_ref, norm_ref, inv_ref, base_ref, agg_grad_ref, send_ref, keep_ref,
    table, aggregate, grads, small, part, halo, weight_ref, weight_out_ref,
    ordered_ref, npart_ref, nweight_ref, nweight_out_ref, ncot_ref, sems
):
    step = pl.program_id(0)
    nodes, width = ordered_ref.shape
    slots = halo.shape[0]
    tiles, tile = part.shape[:2]

    def fetch(number, src, dst):
        return pltpu.make_async_copy(src, dst, sems.at[number])

    def part_fetch(number):
        start = pl.multiple_of(number * tile, tile)
        return fetch(number, part_hbm.at[pl.ds(start, tile), :], part.at[number])

    first = [
        fetch(tiles, halo_hbm, halo),
        fetch(tiles + 1, weight_hbm.at[pl.ds(width, width), :], weight_ref),
        fetch(tiles + 2, weight_out_hbm, weight_out_ref),
    ]
    late = [
        fetch(tiles + 3, ordered_hbm, ordered_ref),
        fetch(tiles + 4, npart_hbm, npart_ref),
        fetch(tiles + 5, nweight_hbm, nweight_ref),
        fetch(tiles + 6, nweight_out_hbm, nweight_out_ref),
        fetch(tiles + 7, ncot_hbm, ncot_ref),
    ]

    @pl.when(step == 0)
    def _():
        first[0].start()
        first[1].start()
        part_fetch(0).start()
        first[2].start()
        for number in range(1, tiles):
            part_fetch(number).start()
        for copy in late:
            copy.start()
        aggregate[...] = jnp.zeros_like(aggregate)
        first[0].wait()
        first[1].wait()
        table[...] = nn(halo[...], weight_ref[...]).astype(BF16)
        first[2].wait()

    part_fetch(step).wait()
    pre = part[step] + tn(pick_columns(rows_ref[0:1, :], slots, nodes), table[...])
    act, slope = activate(pre)
    act = act.astype(BF16)
    act_ref[...] = act
    slope_ref[...] = slope.astype(BF16)
    normed, inv = layer_norm(nn(act, weight_out_ref[...]))
    norm_ref[...] = normed.astype(BF16)
    inv_ref[...] = inv
    message = (normed * gain_ref[...]).astype(BF16)
    aggregate[...] += nn(pick_columns(rows_ref[1:2, :], nodes), message)

    @pl.when(step == pl.num_programs(0) - 1)
    def _():
        for copy in late:
            copy.wait()
        received = aggregate[...].astype(BF16)
        node_act, node_slope = activate(npart_ref[...] + nn(received, nweight_ref[width:]))
        node_act = node_act.astype(BF16)
        node_norm, node_inv = layer_norm(nn(node_act, nweight_out_ref[...]))
        cot = ncot_ref[...].astype(F32)
        small[...] = jnp.zeros_like(small)
        small[3:4] = jnp.sum(cot * node_norm, axis=0, keepdims=True)
        grad_norm = norm_backward(cot * ngain_ref[...], node_norm, node_inv).astype(BF16)
        grad_pre = (nt(grad_norm, nweight_out_ref[...]) * node_slope).astype(BF16)
        small[2:3] = jnp.sum(grad_pre.astype(F32), axis=0, keepdims=True)
        agg_grad_ref[...] = nt(grad_pre, nweight_ref[width:]).astype(BF16)
        base_ref[...] = cot + nt(grad_pre, nweight_ref[:width])
        received = nn(received, permutation(width, 8, SHARE_NODE_IN)).astype(BF16)
        node_act = nn(node_act, permutation(width, 16, SHARE_NODE_OUT)).astype(BF16)
        grads[0] = tn(ordered_ref[...], grad_pre).reshape(STATES, 2, 64, width)
        grads[1] = tn(received, grad_pre).reshape(STATES, 2, 64, width)
        grads[2] = tn(node_act, grad_norm).reshape(STATES, 2, 64, width)
        for dst, side in ((send_ref, 1 - core_ref[0]), (keep_ref, core_ref[0])):
            for state in range(STATES):
                for kind in range(3):
                    row = state * SHARE_NODE + kind * 64
                    dst[row : row + 64, :] = grads[kind, state, side].astype(BF16)
            dst[STATES * SHARE_NODE :, :] = small[...].astype(BF16)


def backward_kernel(
    core_ref, ecot_ref, rows_ref, act_ref, slope_ref, norm_ref, inv_ref, edge_ref,
    agg_grad_ref, gain_ref, weight_out_ref, hidden_ref, halo_hbm, weight_hbm,
    pre_grad_hbm, send_ref, keep_ref, sums_ref, terms_ref,
    grad_in, grad_out, sums, small, halo_ref, weight_ref, held, sems
):
    step = pl.program_id(0)
    nodes, width = hidden_ref.shape
    slots = halo_ref.shape[0]
    tiles, tile = held.shape[:2]
    halo_fetch = pltpu.make_async_copy(halo_hbm, halo_ref, sems.at[tiles])
    weight_fetch = pltpu.make_async_copy(
        weight_hbm.at[pl.ds(width, width), :], weight_ref, sems.at[tiles + 1]
    )

    def push(number):
        start = pl.multiple_of(number * tile, tile)
        return pltpu.make_async_copy(
            held.at[number], pre_grad_hbm.at[pl.ds(start, tile), :], sems.at[number]
        )

    @pl.when(step == 0)
    def _():
        halo_fetch.start()
        weight_fetch.start()
        grad_in[...] = jnp.zeros_like(grad_in)
        grad_out[...] = jnp.zeros_like(grad_out)
        sums[...] = jnp.zeros_like(sums)
        small[...] = jnp.zeros_like(small)

    receivers = pick_columns(rows_ref[1:2, :], nodes)
    message_grad = ecot_ref[...].astype(F32) + tn(receivers, agg_grad_ref[...])
    normed = norm_ref[...].astype(F32)
    small[1:2] += jnp.sum(message_grad * normed, axis=0, keepdims=True)
    grad_norm = norm_backward(message_grad * gain_ref[...], normed, inv_ref[...]).astype(BF16)
    grad_pre = nt(grad_norm, weight_out_ref[...]) * slope_ref[...].astype(F32)
    grad_pre = grad_pre.astype(BF16)
    held[step] = grad_pre
    push(step).start()
    small[0:1] += jnp.sum(grad_pre.astype(F32), axis=0, keepdims=True)
    grad_out[...] += tn(act_ref[...], grad_norm)
    grad_in[:width] += tn(edge_ref[...], grad_pre)
    sums[: nodes + slots] += nn(pick_columns(rows_ref[0:1, :], nodes + slots), grad_pre)
    sums[nodes + slots :] += nn(receivers, grad_pre)

    @pl.when(step == pl.num_programs(0) - 1)
    def _():
        halo_fetch.wait()
        weight_fetch.wait()
        own = sums[:nodes].astype(BF16)
        remote = sums[nodes : nodes + slots].astype(BF16)
        received = sums[nodes + slots :].astype(BF16)
        sums_ref[:nodes] = own
        sums_ref[nodes:] = received
        terms_ref[...] = nt(remote, weight_ref[...]).astype(BF16)
        hidden = hidden_ref[...]
        grad_in[width : 2 * width] = tn(hidden, own) + tn(halo_ref[...], remote)
        grad_in[2 * width :] = tn(hidden, received)
        core = core_ref[0]
        for dst, side in ((send_ref, 1 - core), (keep_ref, core)):

            def pack(chip, carry):
                piece = chip * 2 + side
                row = pl.multiple_of(chip * EDGE_BLOCK, EDGE_BLOCK)
                start = pl.multiple_of(piece * EDGE_IN, EDGE_IN)
                dst[pl.ds(row, EDGE_IN), :] = grad_in[pl.ds(start, EDGE_IN), :].astype(BF16)
                row = pl.multiple_of(row + EDGE_IN, EDGE_OUT)
                start = pl.multiple_of(piece * EDGE_OUT, EDGE_OUT)
                dst[pl.ds(row, EDGE_OUT), :] = grad_out[pl.ds(start, EDGE_OUT), :].astype(BF16)
                return carry

            lax.fori_loop(0, 16, pack, 0, unroll=4)
            dst[16 * EDGE_BLOCK :, :] = small[...].astype(BF16)
        for number in range(tiles):
            push(number).wait()


def pair_kernel(
    batch_ref, keep_ref, recv_ref, nkeep_ref, nrecv_ref,
    mine_ref, one_ref, two_ref, three_ref, states
):
    def both(start, count):
        rows = slice(start, start + count)
        return keep_ref[rows, :].astype(F32) + recv_ref[rows, :].astype(F32)

    def node_both(start, count):
        rows = slice(start, start + count)
        return nkeep_ref[rows, :].astype(F32) + nrecv_ref[rows, :].astype(F32)

    for chip in range(16):
        start = chip * EDGE_BLOCK
        into, out = both(start, EDGE_IN), both(start + EDGE_IN, EDGE_OUT)
        row = chip * SHARE_EDGE
        for state in range(STATES):
            states[state, row : row + SHARE_EDGE_IN, :] = into[
                state * SHARE_EDGE_IN : (state + 1) * SHARE_EDGE_IN
            ]
            states[state, row + SHARE_EDGE_IN : row + SHARE_EDGE, :] = out[
                state * SHARE_EDGE_OUT : (state + 1) * SHARE_EDGE_OUT
            ]
    small = both(16 * EDGE_BLOCK, SMALL) + node_both(STATES * SHARE_NODE, SMALL)
    for state in range(STATES):
        states[state, 16 * SHARE_EDGE : SHARE_ROWS, :] = node_both(state * SHARE_NODE, SHARE_NODE)
        states[state, SHARE_ROWS:, :] = small
    for away, ref in enumerate((mine_ref, one_ref, two_ref, three_ref)):
        ref[...] = states[lax.rem(batch_ref[0] + away, STATES)].astype(BF16)


def merge_kernel(mine_ref, one_ref, two_ref, three_ref, out_ref, block):
    total = (
        mine_ref[...].astype(F32)
        + one_ref[...].astype(F32)
        + two_ref[...].astype(F32)
        + three_ref[...].astype(F32)
    )
    chips, _, width = block.shape
    block[:, :16, :] = total[:256].reshape(chips, 16, width)
    block[:, 16:24, :] = total[256:384].reshape(chips, 8, width)
    for chip in range(chips):
        block[chip, 24:28, :] = total[384 + chip * 4 : 388 + chip * 4]
        block[chip, 28:32, :] = total[SHARE_ROWS : SHARE_ROWS + 4]
    out_ref[...] = block[...].astype(BF16)


def edge_out_kernel(ecot_ref, pre_grad_ref, weight_ref, out_ref):
    out_ref[...] = (
        ecot_ref[...].astype(F32) + nt(pre_grad_ref[...], weight_ref[...])
    ).astype(BF16)


def nodes_kernel(halo_ref, rows_ref, sums_ref, weight_ref, base_ref, out_ref):
    nodes, width = base_ref.shape
    picks = pick_columns(rows_ref[...], nodes)
    out_ref[...] = (
        base_ref[...]
        + nt(sums_ref[:nodes], weight_ref[width : 2 * width])
        + nt(sums_ref[nodes:], weight_ref[2 * width :])
        + nn(picks, halo_ref[...])
    ).astype(BF16)


def finish_kernel(factor, arrived_ref, edge_in_ref, edge_out_ref, node_in_ref, node_out_ref, small_ref):
    total = jnp.sum(arrived_ref[...].astype(F32), axis=0) * factor
    row = 0
    for ref in (edge_in_ref, edge_out_ref, node_in_ref, node_out_ref, small_ref):
        count = ref.shape[0]
        ref[...] = total[row : row + count, :]
        row += count


def call(body, outs, grid=None, in_specs=None, out_specs=None, scratch=(), cost=None, limit=None):
    args = {}
    if grid is not None:
        args = dict(grid=grid, in_specs=in_specs, out_specs=out_specs)
    elif in_specs is not None:
        args = dict(in_specs=in_specs)
    return pl.pallas_call(
        body,
        out_shape=outs,
        scratch_shapes=scratch,
        compiler_params=pltpu.CompilerParams(vmem_limit_bytes=limit or VMEM_MOST),
        cost_estimate=cost,
        **args,
    )


def flops(count, moved):
    return pl.CostEstimate(flops=int(count), bytes_accessed=int(moved), transcendentals=0)


def shape(*dims, dtype=BF16):
    return jax.ShapeDtypeStruct(dims, dtype)


def far(*dims, dtype=BF16):
    return pltpu.HBM(dims, dtype)


def keep_far(*arrays):
    return [pltpu.with_memory_space_constraint(item, pltpu.HBM) for item in arrays]


def full(*dims):
    return pl.BlockSpec(dims, lambda i: (0,) * len(dims))


def tiled(*dims):
    return pl.BlockSpec(dims, lambda i: (i,) + (0,) * (len(dims) - 1))


SCALAR = pl.BlockSpec(memory_space=pltpu.SMEM)
FAR = pl.BlockSpec(memory_space=pltpu.HBM)
WHOLE = pl.BlockSpec(memory_space=pltpu.VMEM)


def shards(
    node_latents, edge_latents, node_cotangent, edge_cotangent, senders, receivers, send_rows,
    edge_weight_in, edge_bias, edge_weight_out, edge_gain,
    node_weight_in, node_bias, node_weight_out, node_gain,
):
    nodes, width = node_latents.shape[1:]
    edges = edge_latents.shape[1]
    parts = lax.axis_size("nodes")
    batch_size = lax.axis_size("batch")
    slots = send_rows.shape[1] * send_rows.shape[2]
    hidden = node_latents[0]
    edge_rows = edge_latents[0]
    ncot = node_cotangent[0]
    ecot = edge_cotangent[0]
    node_index = lax.axis_index("nodes")
    core = jnp.reshape(node_index % 2, (1,)).astype(jnp.int32)
    batch = jnp.reshape(lax.axis_index("batch"), (1,)).astype(jnp.int32)
    tile = min(TILE, edges)
    grid = (edges // tile,)

    row = lambda vector: vector.reshape(1, width)
    index_rows = jnp.stack([senders, receivers], axis=0)

    partner = [(i, i ^ batch_size) for i in range(parts * batch_size)]
    places = [
        [(n * batch_size + b, n * batch_size + (b + away) % batch_size)
         for n in range(parts) for b in range(batch_size)]
        for away in (1, 2, 3)
    ]

    with jax.named_scope("halo_rows"):
        outgoing = call(gather_kernel, shape(slots, width))(send_rows[0].T, hidden)
        halo = lax.all_to_all(
            outgoing.reshape(parts, -1, width), "nodes", 0, 0, tiled=True
        ).reshape(slots, width)
    rows_tile = pl.BlockSpec((2, tile), lambda i: (0, i))
    edge_tile = tiled(tile, width)
    node_full = full(nodes, width)
    node_f32 = shape(nodes, width, dtype=F32)
    with jax.named_scope("edge_pre_local"):
        part, npart, ordered = call(
            local_kernel,
            (far(edges, width, dtype=F32), far(nodes, width, dtype=F32), far(nodes, width)),
            grid,
            [
                edge_tile, rows_tile, node_full, full(3 * width, width), full(1, width),
                full(width, width), full(1, width),
            ],
            (edge_tile, node_full, node_full),
            [pltpu.VMEM((2 * nodes, width), BF16)],
            flops(2 * edges * width * 2 * width, 6 * edges * width),
        )(edge_rows, index_rows, hidden, edge_weight_in, row(edge_bias), node_weight_in, row(node_bias))
    with jax.named_scope("forward"):
        node_pair = shape(STATES * SHARE_NODE + SMALL, width)
        act, slope, norm, inv, base, agg_grad, nsend, nkeep = call(
            forward_kernel,
            (
                shape(edges, width), shape(edges, width), shape(edges, width),
                shape(edges, 1, dtype=F32), far(nodes, width, dtype=F32), shape(nodes, width),
                node_pair, far(*node_pair.shape),
            ),
            grid,
            [SCALAR, rows_tile, full(1, width), full(1, width)] + [FAR] * 9,
            (edge_tile, edge_tile, edge_tile, tiled(tile, 1), node_full, node_full)
            + (full(*node_pair.shape),) * 2,
            [
                pltpu.VMEM((slots, width), BF16), pltpu.VMEM((nodes, width), F32),
                pltpu.VMEM((3, STATES, 2, 64, width), F32), pltpu.VMEM((SMALL, width), F32),
                pltpu.VMEM((edges // tile, tile, width), F32), pltpu.VMEM((slots, width), BF16),
                pltpu.VMEM((width, width), BF16), pltpu.VMEM((width, width), BF16),
                pltpu.VMEM((nodes, width), BF16), pltpu.VMEM((nodes, width), F32),
                pltpu.VMEM((2 * width, width), BF16), pltpu.VMEM((width, width), BF16),
                pltpu.VMEM((nodes, width), BF16), pltpu.SemaphoreType.DMA((edges // tile + 8,)),
            ],
            flops(2 * edges * width * 3 * width, 12 * edges * width),
            VMEM_FEW,
        )(
            core, index_rows, row(edge_gain), row(node_gain),
            *keep_far(
                part, halo, edge_weight_in, edge_weight_out, ordered, npart, node_weight_in,
                node_weight_out, ncot,
            ),
        )
    with jax.named_scope("node_weight_pair"):
        nrecv = lax.ppermute(nsend, ALL, partner)
    with jax.named_scope("backward"):
        edge_pair = shape(16 * EDGE_BLOCK + SMALL, width)
        pre_grad, esend, ekeep, sums, terms = call(
            backward_kernel,
            (
                far(edges, width), edge_pair, far(*edge_pair.shape), far(2 * nodes, width),
                far(slots, width),
            ),
            grid,
            [
                SCALAR, edge_tile, rows_tile, edge_tile, edge_tile, edge_tile,
                tiled(tile, 1), edge_tile, node_full, full(1, width), full(width, width),
                node_full, FAR, FAR,
            ],
            (
                FAR, full(*edge_pair.shape), full(*edge_pair.shape),
                full(2 * nodes, width), full(slots, width),
            ),
            [
                pltpu.VMEM((3 * width, width), F32), pltpu.VMEM((width, width), F32),
                pltpu.VMEM((2 * nodes + slots, width), F32), pltpu.VMEM((SMALL, width), F32),
                pltpu.VMEM((slots, width), BF16), pltpu.VMEM((width, width), BF16),
                pltpu.VMEM((edges // tile, tile, width), BF16),
                pltpu.SemaphoreType.DMA((edges // tile + 2,)),
            ],
            flops(2 * edges * width * 6 * width, 14 * edges * width),
            VMEM_FEW,
        )(
            core, ecot, index_rows, act, slope, norm, inv, edge_rows, agg_grad,
            row(edge_gain), edge_weight_out, hidden, *keep_far(halo, edge_weight_in),
        )
    with jax.named_scope("edge_weight_pair"):
        erecv = lax.ppermute(esend, ALL, partner)
    with jax.named_scope("halo_back"):
        back = lax.all_to_all(
            terms.reshape(parts, -1, width), "nodes", 0, 0, tiled=True
        ).reshape(slots, width)
    with jax.named_scope("pair_sum"):
        block = shape(SHARE_ROWS + SMALL, width)
        blocks = call(
            pair_kernel, (block,) * STATES, in_specs=[SCALAR] + [WHOLE] * 4,
            scratch=[pltpu.VMEM((STATES, *block.shape), F32)],
            cost=flops(0, 8 * edges * width), limit=VMEM_FEW,
        )(batch, *keep_far(ekeep), erecv, *keep_far(nkeep), nrecv)
    with jax.named_scope("weight_states"):
        got = [lax.ppermute(item, ALL, perm) for item, perm in zip(blocks[1:], places)]
    with jax.named_scope("grad_edges"):
        grad_edges = call(
            edge_out_kernel,
            shape(edges, width),
            grid,
            [edge_tile, edge_tile, full(width, width)],
            edge_tile,
            cost=flops(2 * edges * width * width, 6 * edges * width), limit=VMEM_FEW,
        )(*keep_far(ecot, pre_grad, edge_weight_in))
    with jax.named_scope("merge"):
        got, grad_edges = lax.optimization_barrier((got, grad_edges))
        sent = call(
            merge_kernel, shape(16, 32, width),
            scratch=[pltpu.VMEM((16, 32, width), F32)], limit=VMEM_FEW,
        )(blocks[0], *got)
    with jax.named_scope("chip_exchange"):
        chips = parts // 2
        groups = [[2 * chip + side for chip in range(chips)] for side in range(2)]
        arrived = lax.all_to_all(sent, "nodes", 0, 0, tiled=True, axis_index_groups=groups)
    with jax.named_scope("grad_nodes"):
        grad_nodes = call(nodes_kernel, shape(nodes, width), limit=VMEM_FEW)(
            back, send_rows.reshape(1, slots), *keep_far(sums, edge_weight_in, base)
        )
    with jax.named_scope("weight_grads"):
        factor = 1.0 / math.sqrt(batch_size * edges * parts)
        edge_in, edge_out, node_in, node_out, small = call(
            functools.partial(finish_kernel, factor),
            (
                shape(12, width, dtype=F32), shape(4, width, dtype=F32), shape(8, width, dtype=F32),
                shape(4, width, dtype=F32), shape(4, width, dtype=F32),
            ),
            limit=VMEM_FEW,
        )(arrived)
        place = node_index * batch_size + lax.axis_index("batch")
        small = lax.dynamic_slice(small, (0, place * 4), (4, 4))
    return (
        grad_nodes[None], grad_edges[None], edge_in, small[0], edge_out, small[1],
        node_in, small[2], node_out, small[3],
    )


def solution(mesh):
    rows = P("batch", "nodes", None)
    split = P(ALL, None)
    return jax.shard_map(
        shards,
        mesh=mesh,
        in_specs=(rows,) * 4 + (P("nodes"), P("nodes"), P("nodes", None, None)) + (P(),) * 8,
        out_specs=(rows, rows) + (split, P(ALL)) * 4,
        check_vma=False,
    )
```

```python
import functools
import math

import jax
import jax.numpy as jnp
from jax import lax
from jax.experimental import pallas as pl
from jax.experimental.pallas import tpu as pltpu
from jax.sharding import PartitionSpec as P

EPS = 1e-05
ALL = ("nodes", "batch")
F32 = jnp.float32
BF16 = jnp.bfloat16
TILE = 1024
EDGE_IN, EDGE_OUT = 48, 16
SHARE_EDGE_IN, SHARE_EDGE_OUT, SHARE_NODE_IN, SHARE_NODE_OUT = 12, 4, 8, 4
EDGE_BLOCK = EDGE_IN + EDGE_OUT
SHARE_EDGE = SHARE_EDGE_IN + SHARE_EDGE_OUT
SHARE_NODE = 192
SHARE_ROWS = 16 * SHARE_EDGE + SHARE_NODE
SMALL = 16
STATES = 4
VMEM_FEW = 24 * 1024 * 1024
VMEM_MOST = 62 * 1024 * 1024


def nn(lhs, rhs):
    return lax.dot_general(lhs, rhs, (((1,), (0,)), ((), ())), preferred_element_type=F32)


def nt(lhs, rhs):
    return lax.dot_general(lhs, rhs, (((1,), (1,)), ((), ())), preferred_element_type=F32)


def tn(lhs, rhs):
    return lax.dot_general(lhs, rhs, (((0,), (0,)), ((), ())), preferred_element_type=F32)


def pick_rows(index_column, count, first=0):
    shape = (index_column.shape[0], count)
    columns = lax.broadcasted_iota(jnp.int32, shape, 1) + first
    return jnp.where(index_column == columns, 1.0, 0.0).astype(BF16)


def pick_columns(index_row, count, first=0):
    shape = (count, index_row.shape[1])
    rows = lax.broadcasted_iota(jnp.int32, shape, 0) + first
    return jnp.where(index_row == rows, 1.0, 0.0).astype(BF16)


def activate(pre):
    sig = jax.nn.sigmoid(pre)
    return pre * sig, sig * (1.0 + pre * (1.0 - sig))


def layer_norm(pre_norm):
    centred = pre_norm - jnp.mean(pre_norm, axis=-1, keepdims=True)
    inv = lax.rsqrt(jnp.mean(centred * centred, axis=-1, keepdims=True) + EPS)
    return centred * inv, inv


def norm_backward(scaled, normed, inv):
    mean_scaled = jnp.mean(scaled, axis=-1, keepdims=True)
    mean_product = jnp.mean(scaled * normed, axis=-1, keepdims=True)
    return (scaled - mean_scaled - normed * mean_product) * inv


def permutation(count, shares, rows):
    source = lax.broadcasted_iota(jnp.int32, (count, count), 0)
    place = lax.broadcasted_iota(jnp.int32, (count, count), 1)
    row = place % rows
    chip = (place // rows) % shares
    core = (place // (rows * shares)) % 2
    state = place // (rows * shares * 2)
    wanted = ((chip * 2 + core) * STATES + state) * rows + row
    return jnp.where(source == wanted, 1.0, 0.0).astype(BF16)


def gather_kernel(rows_ref, hidden_ref, out_ref):
    slots, peers = rows_ref.shape
    lists = rows_ref[...].astype(F32).astype(BF16)
    place = lax.broadcasted_iota(jnp.int32, (peers * slots, slots), 0)
    slot = lax.broadcasted_iota(jnp.int32, (peers * slots, slots), 1)
    spread = nn(jnp.where(place % slots == slot, 1.0, 0.0).astype(BF16), lists)
    place = lax.broadcasted_iota(jnp.int32, (peers * slots, peers), 0)
    peer = lax.broadcasted_iota(jnp.int32, (peers * slots, peers), 1)
    column = jnp.sum(
        jnp.where(place // slots == peer, spread, 0.0), axis=1, keepdims=True
    ).astype(jnp.int32)
    out_ref[...] = nn(pick_rows(column, hidden_ref.shape[0]), hidden_ref[...]).astype(BF16)


def local_kernel(
    edge_ref, rows_ref, hidden_ref, weight_ref, bias_ref, nweight_ref, nbias_ref,
    part_ref, npart_ref, ordered_ref, table
):
    width = hidden_ref.shape[1]
    nodes = hidden_ref.shape[0]

    @pl.when(pl.program_id(0) == 0)
    def _():
        hidden = hidden_ref[...]
        table[:nodes] = nn(hidden, weight_ref[width : 2 * width]).astype(BF16)
        table[nodes:] = nn(hidden, weight_ref[2 * width :]).astype(BF16)
        npart_ref[...] = nn(hidden, nweight_ref[...]) + nbias_ref[...]
        ordered_ref[...] = nn(hidden, permutation(width, 8, SHARE_NODE_IN)).astype(BF16)

    picks = jnp.concatenate(
        [pick_columns(rows_ref[0:1, :], nodes), pick_columns(rows_ref[1:2, :], nodes)], axis=0
    )
    part_ref[...] = (
        nn(edge_ref[...], weight_ref[:width]) + tn(picks, table[...]) + bias_ref[...]
    )


def forward_kernel(
    core_ref, rows_ref, gain_ref, ngain_ref, part_hbm, halo_hbm, weight_hbm, weight_out_hbm,
    ordered_hbm, npart_hbm, nweight_hbm, nweight_out_hbm, ncot_hbm,
    act_ref, slope_ref, norm_ref, inv_ref, base_ref, agg_grad_ref, send_ref, keep_ref,
    table, aggregate, grads, small, part, halo, weight_ref, weight_out_ref,
    ordered_ref, npart_ref, nweight_ref, nweight_out_ref, ncot_ref, sems
):
    nodes, width = ordered_ref.shape
    slots = halo.shape[0]
    tiles, tile = part.shape[:2]

    def fetch(number, src, dst):
        return pltpu.make_async_copy(src, dst, sems.at[number])

    def part_fetch(number):
        return fetch(number, part_hbm.at[pl.ds(number * tile, tile), :], part.at[number])

    first = [
        fetch(tiles, halo_hbm, halo),
        fetch(tiles + 1, weight_hbm.at[pl.ds(width, width), :], weight_ref),
        fetch(tiles + 2, weight_out_hbm, weight_out_ref),
    ]
    late = [
        fetch(tiles + 3, ordered_hbm, ordered_ref),
        fetch(tiles + 4, npart_hbm, npart_ref),
        fetch(tiles + 5, nweight_hbm, nweight_ref),
        fetch(tiles + 6, nweight_out_hbm, nweight_out_ref),
        fetch(tiles + 7, ncot_hbm, ncot_ref),
    ]

    first[0].start()
    first[1].start()
    part_fetch(0).start()
    first[2].start()
    for number in range(1, tiles):
        part_fetch(number).start()
    for copy in late:
        copy.start()
    first[0].wait()
    first[1].wait()
    table[...] = nn(halo[...], weight_ref[...]).astype(BF16)
    for step in range(tiles):
        rows = slice(step * tile, (step + 1) * tile)
        part_fetch(step).wait()
        pre = part[step] + tn(pick_columns(rows_ref[0:1, rows], slots, nodes), table[...])
        act, slope = activate(pre)
        act = act.astype(BF16)
        act_ref[rows, :] = act
        slope_ref[rows, :] = slope.astype(BF16)
        if step == 0:
            first[2].wait()
        normed, inv = layer_norm(nn(act, weight_out_ref[...]))
        norm_ref[rows, :] = normed.astype(BF16)
        inv_ref[rows, :] = inv
        message = (normed * gain_ref[...]).astype(BF16)
        added = nn(pick_columns(rows_ref[1:2, rows], nodes), message)
        if step == 0:
            aggregate[...] = added
        else:
            aggregate[...] += added
    for copy in late:
        copy.wait()
    received = aggregate[...].astype(BF16)
    node_act, node_slope = activate(npart_ref[...] + nn(received, nweight_ref[width:]))
    node_act = node_act.astype(BF16)
    node_norm, node_inv = layer_norm(nn(node_act, nweight_out_ref[...]))
    cot = ncot_ref[...].astype(F32)
    small[...] = jnp.zeros_like(small)
    small[3:4] = jnp.sum(cot * node_norm, axis=0, keepdims=True)
    grad_norm = norm_backward(cot * ngain_ref[...], node_norm, node_inv).astype(BF16)
    grad_pre = (nt(grad_norm, nweight_out_ref[...]) * node_slope).astype(BF16)
    small[2:3] = jnp.sum(grad_pre.astype(F32), axis=0, keepdims=True)
    agg_grad_ref[...] = nt(grad_pre, nweight_ref[width:]).astype(BF16)
    base_ref[...] = cot + nt(grad_pre, nweight_ref[:width])
    received = nn(received, permutation(width, 8, SHARE_NODE_IN)).astype(BF16)
    node_act = nn(node_act, permutation(width, 16, SHARE_NODE_OUT)).astype(BF16)
    grads[0] = tn(ordered_ref[...], grad_pre).reshape(STATES, 2, 64, width)
    grads[1] = tn(received, grad_pre).reshape(STATES, 2, 64, width)
    grads[2] = tn(node_act, grad_norm).reshape(STATES, 2, 64, width)
    for dst, side in ((send_ref, 1 - core_ref[0]), (keep_ref, core_ref[0])):
        for state in range(STATES):
            for kind in range(3):
                row = state * SHARE_NODE + kind * 64
                dst[row : row + 64, :] = grads[kind, state, side].astype(BF16)
        dst[STATES * SHARE_NODE :, :] = small[...].astype(BF16)


def backward_kernel(
    core_ref, ecot_ref, rows_ref, act_ref, slope_ref, norm_ref, inv_ref, edge_ref,
    agg_grad_ref, gain_ref, weight_out_ref, hidden_ref, halo_hbm, weight_hbm,
    pre_grad_hbm, send_ref, keep_ref, sums_ref, terms_ref,
    grad_in, grad_out, sums, small, halo_ref, weight_ref, held, sems
):
    nodes, width = hidden_ref.shape
    slots = halo_ref.shape[0]
    tiles, tile = held.shape[:2]
    halo_fetch = pltpu.make_async_copy(halo_hbm, halo_ref, sems.at[tiles])
    weight_fetch = pltpu.make_async_copy(
        weight_hbm.at[pl.ds(width, width), :], weight_ref, sems.at[tiles + 1]
    )

    def push(number):
        return pltpu.make_async_copy(
            held.at[number], pre_grad_hbm.at[pl.ds(number * tile, tile), :], sems.at[number]
        )

    halo_fetch.start()
    weight_fetch.start()
    small[...] = jnp.zeros_like(small)
    for step in range(tiles):
        rows = slice(step * tile, (step + 1) * tile)

        def add(ref, place, value):
            if step == 0:
                ref[place] = value
            else:
                ref[place] += value

        receivers = pick_columns(rows_ref[1:2, rows], nodes)
        message_grad = ecot_ref[rows, :].astype(F32) + tn(receivers, agg_grad_ref[...])
        normed = norm_ref[rows, :].astype(F32)
        small[1:2] += jnp.sum(message_grad * normed, axis=0, keepdims=True)
        grad_norm = norm_backward(
            message_grad * gain_ref[...], normed, inv_ref[rows, :]
        ).astype(BF16)
        grad_pre = nt(grad_norm, weight_out_ref[...]) * slope_ref[rows, :].astype(F32)
        grad_pre = grad_pre.astype(BF16)
        held[step] = grad_pre
        push(step).start()
        small[0:1] += jnp.sum(grad_pre.astype(F32), axis=0, keepdims=True)
        add(grad_out, slice(None), tn(act_ref[rows, :], grad_norm))
        add(grad_in, slice(0, width), tn(edge_ref[rows, :], grad_pre))
        senders = pick_columns(rows_ref[0:1, rows], nodes + slots)
        add(sums, slice(0, nodes + slots), nn(senders, grad_pre))
        add(sums, slice(nodes + slots, None), nn(receivers, grad_pre))
    halo_fetch.wait()
    weight_fetch.wait()
    own = sums[:nodes].astype(BF16)
    remote = sums[nodes : nodes + slots].astype(BF16)
    received = sums[nodes + slots :].astype(BF16)
    sums_ref[:nodes] = own
    sums_ref[nodes:] = received
    terms_ref[...] = nt(remote, weight_ref[...]).astype(BF16)
    hidden = hidden_ref[...]
    grad_in[width : 2 * width] = tn(hidden, own) + tn(halo_ref[...], remote)
    grad_in[2 * width :] = tn(hidden, received)
    core = core_ref[0]
    for dst, side in ((send_ref, 1 - core), (keep_ref, core)):

        def pack(chip, carry):
            piece = chip * 2 + side
            row = pl.multiple_of(chip * EDGE_BLOCK, EDGE_BLOCK)
            start = pl.multiple_of(piece * EDGE_IN, EDGE_IN)
            dst[pl.ds(row, EDGE_IN), :] = grad_in[pl.ds(start, EDGE_IN), :].astype(BF16)
            row = pl.multiple_of(row + EDGE_IN, EDGE_OUT)
            start = pl.multiple_of(piece * EDGE_OUT, EDGE_OUT)
            dst[pl.ds(row, EDGE_OUT), :] = grad_out[pl.ds(start, EDGE_OUT), :].astype(BF16)
            return carry

        lax.fori_loop(0, 16, pack, 0, unroll=4)
        dst[16 * EDGE_BLOCK :, :] = small[...].astype(BF16)
    for number in range(tiles):
        push(number).wait()


def pair_kernel(
    batch_ref, keep_ref, recv_ref, nkeep_ref, nrecv_ref,
    mine_ref, one_ref, two_ref, three_ref, states
):
    def both(start, count):
        rows = slice(start, start + count)
        return keep_ref[rows, :].astype(F32) + recv_ref[rows, :].astype(F32)

    def node_both(start, count):
        rows = slice(start, start + count)
        return nkeep_ref[rows, :].astype(F32) + nrecv_ref[rows, :].astype(F32)

    for chip in range(16):
        start = chip * EDGE_BLOCK
        into, out = both(start, EDGE_IN), both(start + EDGE_IN, EDGE_OUT)
        row = chip * SHARE_EDGE
        for state in range(STATES):
            states[state, row : row + SHARE_EDGE_IN, :] = into[
                state * SHARE_EDGE_IN : (state + 1) * SHARE_EDGE_IN
            ]
            states[state, row + SHARE_EDGE_IN : row + SHARE_EDGE, :] = out[
                state * SHARE_EDGE_OUT : (state + 1) * SHARE_EDGE_OUT
            ]
    small = both(16 * EDGE_BLOCK, SMALL) + node_both(STATES * SHARE_NODE, SMALL)
    for state in range(STATES):
        states[state, 16 * SHARE_EDGE : SHARE_ROWS, :] = node_both(state * SHARE_NODE, SHARE_NODE)
        states[state, SHARE_ROWS:, :] = small
    for away, ref in enumerate((mine_ref, one_ref, two_ref, three_ref)):
        ref[...] = states[lax.rem(batch_ref[0] + away, STATES)].astype(BF16)


def merge_kernel(mine_ref, one_ref, two_ref, three_ref, out_ref, block):
    total = (
        mine_ref[...].astype(F32)
        + one_ref[...].astype(F32)
        + two_ref[...].astype(F32)
        + three_ref[...].astype(F32)
    )
    chips, _, width = block.shape
    block[:, :16, :] = total[:256].reshape(chips, 16, width)
    block[:, 16:24, :] = total[256:384].reshape(chips, 8, width)
    for chip in range(chips):
        block[chip, 24:28, :] = total[384 + chip * 4 : 388 + chip * 4]
        block[chip, 28:32, :] = total[SHARE_ROWS : SHARE_ROWS + 4]
    out_ref[...] = block[...].astype(BF16)


def edge_out_kernel(ecot_ref, pre_grad_ref, weight_ref, out_ref):
    out_ref[...] = (
        ecot_ref[...].astype(F32) + nt(pre_grad_ref[...], weight_ref[...])
    ).astype(BF16)


def nodes_kernel(halo_ref, rows_ref, sums_ref, weight_ref, base_ref, out_ref):
    nodes, width = base_ref.shape
    picks = pick_columns(rows_ref[...], nodes)
    out_ref[...] = (
        base_ref[...]
        + nt(sums_ref[:nodes], weight_ref[width : 2 * width])
        + nt(sums_ref[nodes:], weight_ref[2 * width :])
        + nn(picks, halo_ref[...])
    ).astype(BF16)


def finish_kernel(factor, arrived_ref, edge_in_ref, edge_out_ref, node_in_ref, node_out_ref, small_ref):
    total = jnp.sum(arrived_ref[...].astype(F32), axis=0) * factor
    row = 0
    for ref in (edge_in_ref, edge_out_ref, node_in_ref, node_out_ref, small_ref):
        count = ref.shape[0]
        ref[...] = total[row : row + count, :]
        row += count


def call(body, outs, grid=None, in_specs=None, out_specs=None, scratch=(), cost=None, limit=None):
    args = {}
    if grid is not None:
        args = dict(grid=grid, in_specs=in_specs, out_specs=out_specs)
    elif in_specs is not None:
        args = dict(in_specs=in_specs)
        if out_specs is not None:
            args["out_specs"] = tuple(out_specs)
    return pl.pallas_call(
        body,
        out_shape=outs,
        scratch_shapes=scratch,
        compiler_params=pltpu.CompilerParams(vmem_limit_bytes=limit or VMEM_MOST),
        cost_estimate=cost,
        **args,
    )


def flops(count, moved):
    return pl.CostEstimate(flops=int(count), bytes_accessed=int(moved), transcendentals=0)


def shape(*dims, dtype=BF16):
    return jax.ShapeDtypeStruct(dims, dtype)


def far(*dims, dtype=BF16):
    return pltpu.HBM(dims, dtype)


def keep_far(*arrays):
    return [pltpu.with_memory_space_constraint(item, pltpu.HBM) for item in arrays]


def full(*dims):
    return pl.BlockSpec(dims, lambda i: (0,) * len(dims))


def tiled(*dims):
    return pl.BlockSpec(dims, lambda i: (i,) + (0,) * (len(dims) - 1))


SCALAR = pl.BlockSpec(memory_space=pltpu.SMEM)
FAR = pl.BlockSpec(memory_space=pltpu.HBM)
WHOLE = pl.BlockSpec(memory_space=pltpu.VMEM)


def shards(
    node_latents, edge_latents, node_cotangent, edge_cotangent, senders, receivers, send_rows,
    edge_weight_in, edge_bias, edge_weight_out, edge_gain,
    node_weight_in, node_bias, node_weight_out, node_gain,
):
    nodes, width = node_latents.shape[1:]
    edges = edge_latents.shape[1]
    parts = lax.axis_size("nodes")
    batch_size = lax.axis_size("batch")
    slots = send_rows.shape[1] * send_rows.shape[2]
    hidden = node_latents[0]
    edge_rows = edge_latents[0]
    ncot = node_cotangent[0]
    ecot = edge_cotangent[0]
    node_index = lax.axis_index("nodes")
    core = jnp.reshape(node_index % 2, (1,)).astype(jnp.int32)
    batch = jnp.reshape(lax.axis_index("batch"), (1,)).astype(jnp.int32)
    tile = min(TILE, edges)
    grid = (edges // tile,)

    row = lambda vector: vector.reshape(1, width)
    index_rows = jnp.stack([senders, receivers], axis=0)

    partner = [(i, i ^ batch_size) for i in range(parts * batch_size)]
    places = [
        [(n * batch_size + b, n * batch_size + (b + away) % batch_size)
         for n in range(parts) for b in range(batch_size)]
        for away in (1, 2, 3)
    ]

    with jax.named_scope("halo_rows"):
        outgoing = call(gather_kernel, shape(slots, width))(send_rows[0].T, hidden)
        halo = lax.all_to_all(
            outgoing.reshape(parts, -1, width), "nodes", 0, 0, tiled=True
        ).reshape(slots, width)
    rows_tile = pl.BlockSpec((2, tile), lambda i: (0, i))
    edge_tile = tiled(tile, width)
    node_full = full(nodes, width)
    node_f32 = shape(nodes, width, dtype=F32)
    with jax.named_scope("edge_pre_local"):
        part, npart, ordered = call(
            local_kernel,
            (far(edges, width, dtype=F32), far(nodes, width, dtype=F32), far(nodes, width)),
            grid,
            [
                edge_tile, rows_tile, node_full, full(3 * width, width), full(1, width),
                full(width, width), full(1, width),
            ],
            (edge_tile, node_full, node_full),
            [pltpu.VMEM((2 * nodes, width), BF16)],
            flops(2 * edges * width * 2 * width, 6 * edges * width),
        )(edge_rows, index_rows, hidden, edge_weight_in, row(edge_bias), node_weight_in, row(node_bias))
    with jax.named_scope("forward"):
        node_pair = shape(STATES * SHARE_NODE + SMALL, width)
        act, slope, norm, inv, base, agg_grad, nsend, nkeep = call(
            forward_kernel,
            (
                shape(edges, width), shape(edges, width), shape(edges, width),
                shape(edges, 1, dtype=F32), far(nodes, width, dtype=F32), shape(nodes, width),
                node_pair, far(*node_pair.shape),
            ),
            None,
            [SCALAR, WHOLE, WHOLE, WHOLE] + [FAR] * 9,
            None,
            [
                pltpu.VMEM((slots, width), BF16), pltpu.VMEM((nodes, width), F32),
                pltpu.VMEM((3, STATES, 2, 64, width), F32), pltpu.VMEM((SMALL, width), F32),
                pltpu.VMEM((edges // tile, tile, width), F32), pltpu.VMEM((slots, width), BF16),
                pltpu.VMEM((width, width), BF16), pltpu.VMEM((width, width), BF16),
                pltpu.VMEM((nodes, width), BF16), pltpu.VMEM((nodes, width), F32),
                pltpu.VMEM((2 * width, width), BF16), pltpu.VMEM((width, width), BF16),
                pltpu.VMEM((nodes, width), BF16), pltpu.SemaphoreType.DMA((edges // tile + 8,)),
            ],
            flops(2 * edges * width * 3 * width, 12 * edges * width),
            VMEM_FEW,
        )(
            core, index_rows, row(edge_gain), row(node_gain),
            *keep_far(
                part, halo, edge_weight_in, edge_weight_out, ordered, npart, node_weight_in,
                node_weight_out, ncot,
            ),
        )
    with jax.named_scope("node_weight_pair"):
        nrecv = lax.ppermute(nsend, ALL, partner)
    with jax.named_scope("backward"):
        edge_pair = shape(16 * EDGE_BLOCK + SMALL, width)
        pre_grad, esend, ekeep, sums, terms = call(
            backward_kernel,
            (
                far(edges, width), edge_pair, far(*edge_pair.shape), far(2 * nodes, width),
                far(slots, width),
            ),
            None,
            [SCALAR] + [WHOLE] * 11 + [FAR, FAR],
            [FAR] + [WHOLE] * 4,
            [
                pltpu.VMEM((3 * width, width), F32), pltpu.VMEM((width, width), F32),
                pltpu.VMEM((2 * nodes + slots, width), F32), pltpu.VMEM((SMALL, width), F32),
                pltpu.VMEM((slots, width), BF16), pltpu.VMEM((width, width), BF16),
                pltpu.VMEM((edges // tile, tile, width), BF16),
                pltpu.SemaphoreType.DMA((edges // tile + 2,)),
            ],
            flops(2 * edges * width * 6 * width, 14 * edges * width),
            VMEM_FEW,
        )(
            core, ecot, index_rows, act, slope, norm, inv, edge_rows, agg_grad,
            row(edge_gain), edge_weight_out, hidden, *keep_far(halo, edge_weight_in),
        )
    with jax.named_scope("edge_weight_pair"):
        erecv = lax.ppermute(esend, ALL, partner)
    with jax.named_scope("halo_back"):
        back = lax.all_to_all(
            terms.reshape(parts, -1, width), "nodes", 0, 0, tiled=True
        ).reshape(slots, width)
    with jax.named_scope("pair_sum"):
        block = shape(SHARE_ROWS + SMALL, width)
        blocks = call(
            pair_kernel, (block,) * STATES, in_specs=[SCALAR] + [WHOLE] * 4,
            scratch=[pltpu.VMEM((STATES, *block.shape), F32)],
            cost=flops(0, 8 * edges * width), limit=VMEM_FEW,
        )(batch, *keep_far(ekeep), erecv, *keep_far(nkeep), nrecv)
    with jax.named_scope("weight_states"):
        got = [lax.ppermute(item, ALL, perm) for item, perm in zip(blocks[1:], places)]
    with jax.named_scope("grad_edges"):
        grad_edges = call(
            edge_out_kernel,
            shape(edges, width),
            grid,
            [edge_tile, edge_tile, full(width, width)],
            edge_tile,
            cost=flops(2 * edges * width * width, 6 * edges * width), limit=VMEM_FEW,
        )(*keep_far(ecot, pre_grad, edge_weight_in))
    with jax.named_scope("merge"):
        got, grad_edges = lax.optimization_barrier((got, grad_edges))
        sent = call(
            merge_kernel, shape(16, 32, width),
            scratch=[pltpu.VMEM((16, 32, width), F32)], limit=VMEM_FEW,
        )(blocks[0], *got)
    with jax.named_scope("chip_exchange"):
        chips = parts // 2
        groups = [[2 * chip + side for chip in range(chips)] for side in range(2)]
        arrived = lax.all_to_all(sent, "nodes", 0, 0, tiled=True, axis_index_groups=groups)
    with jax.named_scope("grad_nodes"):
        grad_nodes = call(nodes_kernel, shape(nodes, width), limit=VMEM_FEW)(
            back, send_rows.reshape(1, slots), *keep_far(sums, edge_weight_in, base)
        )
    with jax.named_scope("weight_grads"):
        factor = 1.0 / math.sqrt(batch_size * edges * parts)
        edge_in, edge_out, node_in, node_out, small = call(
            functools.partial(finish_kernel, factor),
            (
                shape(12, width, dtype=F32), shape(4, width, dtype=F32), shape(8, width, dtype=F32),
                shape(4, width, dtype=F32), shape(4, width, dtype=F32),
            ),
            limit=VMEM_FEW,
        )(arrived)
        place = node_index * batch_size + lax.axis_index("batch")
        small = lax.dynamic_slice(small, (0, place * 4), (4, 4))
    return (
        grad_nodes[None], grad_edges[None], edge_in, small[0], edge_out, small[1],
        node_in, small[2], node_out, small[3],
    )


def solution(mesh):
    rows = P("batch", "nodes", None)
    split = P(ALL, None)
    return jax.shard_map(
        shards,
        mesh=mesh,
        in_specs=(rows,) * 4 + (P("nodes"), P("nodes"), P("nodes", None, None)) + (P(),) * 8,
        out_specs=(rows, rows) + (split, P(ALL)) * 4,
        check_vma=False,
    )
```

```python
import functools
import math

import jax
import jax.numpy as jnp
from jax import lax
from jax.experimental import pallas as pl
from jax.experimental.pallas import tpu as pltpu
from jax.sharding import PartitionSpec as P

EPS = 1e-05
ALL = ("nodes", "batch")
F32 = jnp.float32
BF16 = jnp.bfloat16
TILE = 1024
EDGE_IN, EDGE_OUT = 48, 16
SHARE_EDGE_IN, SHARE_EDGE_OUT, SHARE_NODE_IN, SHARE_NODE_OUT = 12, 4, 8, 4
EDGE_BLOCK = EDGE_IN + EDGE_OUT
SHARE_EDGE = SHARE_EDGE_IN + SHARE_EDGE_OUT
SHARE_NODE = 192
SHARE_ROWS = 16 * SHARE_EDGE + SHARE_NODE
SMALL = 16
STATES = 4
VMEM_FEW = 24 * 1024 * 1024
VMEM_MOST = 62 * 1024 * 1024


def nn(lhs, rhs):
    return lax.dot_general(lhs, rhs, (((1,), (0,)), ((), ())), preferred_element_type=F32)


def nt(lhs, rhs):
    return lax.dot_general(lhs, rhs, (((1,), (1,)), ((), ())), preferred_element_type=F32)


def tn(lhs, rhs):
    return lax.dot_general(lhs, rhs, (((0,), (0,)), ((), ())), preferred_element_type=F32)


def pick_rows(index_column, count, first=0):
    shape = (index_column.shape[0], count)
    columns = lax.broadcasted_iota(jnp.int32, shape, 1) + first
    return jnp.where(index_column == columns, 1.0, 0.0).astype(BF16)


def pick_columns(index_row, count, first=0):
    shape = (count, index_row.shape[1])
    rows = lax.broadcasted_iota(jnp.int32, shape, 0) + first
    return jnp.where(index_row == rows, 1.0, 0.0).astype(BF16)


def activate(pre):
    sig = jax.nn.sigmoid(pre)
    return pre * sig, sig * (1.0 + pre * (1.0 - sig))


def layer_norm(pre_norm):
    centred = pre_norm - jnp.mean(pre_norm, axis=-1, keepdims=True)
    inv = lax.rsqrt(jnp.mean(centred * centred, axis=-1, keepdims=True) + EPS)
    return centred * inv, inv


def norm_backward(scaled, normed, inv):
    mean_scaled = jnp.mean(scaled, axis=-1, keepdims=True)
    mean_product = jnp.mean(scaled * normed, axis=-1, keepdims=True)
    return (scaled - mean_scaled - normed * mean_product) * inv


def permutation(count, shares, rows):
    source = lax.broadcasted_iota(jnp.int32, (count, count), 0)
    place = lax.broadcasted_iota(jnp.int32, (count, count), 1)
    row = place % rows
    chip = (place // rows) % shares
    core = (place // (rows * shares)) % 2
    state = place // (rows * shares * 2)
    wanted = ((chip * 2 + core) * STATES + state) * rows + row
    return jnp.where(source == wanted, 1.0, 0.0).astype(BF16)


def gather_kernel(rows_ref, hidden_ref, out_ref):
    slots, peers = rows_ref.shape
    lists = rows_ref[...].astype(F32).astype(BF16)
    place = lax.broadcasted_iota(jnp.int32, (peers * slots, slots), 0)
    slot = lax.broadcasted_iota(jnp.int32, (peers * slots, slots), 1)
    spread = nn(jnp.where(place % slots == slot, 1.0, 0.0).astype(BF16), lists)
    place = lax.broadcasted_iota(jnp.int32, (peers * slots, peers), 0)
    peer = lax.broadcasted_iota(jnp.int32, (peers * slots, peers), 1)
    column = jnp.sum(
        jnp.where(place // slots == peer, spread, 0.0), axis=1, keepdims=True
    ).astype(jnp.int32)
    out_ref[...] = nn(pick_rows(column, hidden_ref.shape[0]), hidden_ref[...]).astype(BF16)


def local_kernel(
    edge_ref, rows_ref, hidden_ref, weight_ref, bias_ref, nweight_ref, nbias_ref,
    part_ref, npart_ref, ordered_ref, table
):
    width = hidden_ref.shape[1]
    nodes = hidden_ref.shape[0]

    @pl.when(pl.program_id(0) == 0)
    def _():
        hidden = hidden_ref[...]
        table[:nodes] = nn(hidden, weight_ref[width : 2 * width]).astype(BF16)
        table[nodes:] = nn(hidden, weight_ref[2 * width :]).astype(BF16)
        npart_ref[...] = nn(hidden, nweight_ref[...]) + nbias_ref[...]
        ordered_ref[...] = nn(hidden, permutation(width, 8, SHARE_NODE_IN)).astype(BF16)

    picks = jnp.concatenate(
        [pick_columns(rows_ref[0:1, :], nodes), pick_columns(rows_ref[1:2, :], nodes)], axis=0
    )
    part_ref[...] = (
        nn(edge_ref[...], weight_ref[:width]) + tn(picks, table[...]) + bias_ref[...]
    )


def forward_kernel(
    core_ref, rows_ref, gain_ref, ngain_ref, part_hbm, halo_hbm, weight_hbm, weight_out_hbm,
    ordered_hbm, npart_hbm, nweight_hbm, nweight_out_hbm, ncot_hbm,
    act_ref, slope_ref, norm_ref, inv_ref, grad_pre_ref, agg_grad_ref, send_ref, keep_ref,
    table, aggregate, grads, small, part, halo, weight_ref, weight_out_ref,
    ordered_ref, npart_ref, nweight_ref, nweight_out_ref, ncot_ref, sems
):
    nodes, width = ordered_ref.shape
    slots = halo.shape[0]
    tiles, tile = part.shape[:2]

    def fetch(number, src, dst):
        return pltpu.make_async_copy(src, dst, sems.at[number])

    def part_fetch(number):
        return fetch(number, part_hbm.at[pl.ds(number * tile, tile), :], part.at[number])

    first = [
        fetch(tiles, halo_hbm, halo),
        fetch(tiles + 1, weight_hbm.at[pl.ds(width, width), :], weight_ref),
        fetch(tiles + 2, weight_out_hbm, weight_out_ref),
    ]
    late = [
        fetch(tiles + 3, ordered_hbm, ordered_ref),
        fetch(tiles + 4, npart_hbm, npart_ref),
        fetch(tiles + 5, nweight_hbm, nweight_ref),
        fetch(tiles + 6, nweight_out_hbm, nweight_out_ref),
        fetch(tiles + 7, ncot_hbm, ncot_ref),
    ]

    first[0].start()
    first[1].start()
    part_fetch(0).start()
    first[2].start()
    for number in range(1, tiles):
        part_fetch(number).start()
    for copy in late:
        copy.start()
    first[0].wait()
    first[1].wait()
    table[...] = nn(halo[...], weight_ref[...]).astype(BF16)
    for step in range(tiles):
        rows = slice(step * tile, (step + 1) * tile)
        part_fetch(step).wait()
        pre = part[step] + tn(pick_columns(rows_ref[0:1, rows], slots, nodes), table[...])
        act, slope = activate(pre)
        act = act.astype(BF16)
        act_ref[rows, :] = act
        slope_ref[rows, :] = slope.astype(BF16)
        if step == 0:
            first[2].wait()
        normed, inv = layer_norm(nn(act, weight_out_ref[...]))
        norm_ref[rows, :] = normed.astype(BF16)
        inv_ref[rows, :] = inv
        message = (normed * gain_ref[...]).astype(BF16)
        added = nn(pick_columns(rows_ref[1:2, rows], nodes), message)
        if step == 0:
            aggregate[...] = added
        else:
            aggregate[...] += added
    for copy in late:
        copy.wait()
    received = aggregate[...].astype(BF16)
    node_act, node_slope = activate(npart_ref[...] + nn(received, nweight_ref[width:]))
    node_act = node_act.astype(BF16)
    node_norm, node_inv = layer_norm(nn(node_act, nweight_out_ref[...]))
    cot = ncot_ref[...].astype(F32)
    small[...] = jnp.zeros_like(small)
    small[3:4] = jnp.sum(cot * node_norm, axis=0, keepdims=True)
    grad_norm = norm_backward(cot * ngain_ref[...], node_norm, node_inv).astype(BF16)
    grad_pre = (nt(grad_norm, nweight_out_ref[...]) * node_slope).astype(BF16)
    small[2:3] = jnp.sum(grad_pre.astype(F32), axis=0, keepdims=True)
    agg_grad_ref[...] = nt(grad_pre, nweight_ref[width:]).astype(BF16)
    grad_pre_ref[...] = grad_pre
    received = nn(received, permutation(width, 8, SHARE_NODE_IN)).astype(BF16)
    node_act = nn(node_act, permutation(width, 16, SHARE_NODE_OUT)).astype(BF16)
    grads[0] = tn(ordered_ref[...], grad_pre).reshape(STATES, 2, 64, width)
    grads[1] = tn(received, grad_pre).reshape(STATES, 2, 64, width)
    grads[2] = tn(node_act, grad_norm).reshape(STATES, 2, 64, width)
    for dst, side in ((send_ref, 1 - core_ref[0]), (keep_ref, core_ref[0])):
        for state in range(STATES):
            for kind in range(3):
                row = state * SHARE_NODE + kind * 64
                dst[row : row + 64, :] = grads[kind, state, side].astype(BF16)
        dst[STATES * SHARE_NODE :, :] = small[...].astype(BF16)


def backward_kernel(
    core_ref, ecot_ref, rows_ref, act_ref, slope_ref, norm_ref, inv_ref, edge_ref,
    agg_grad_ref, gain_ref, weight_out_ref, hidden_ref, halo_hbm, weight_hbm,
    pre_grad_hbm, send_ref, keep_ref, sums_ref, terms_ref,
    grad_in, grad_out, sums, small, halo_ref, weight_ref, held, sems
):
    nodes, width = hidden_ref.shape
    slots = halo_ref.shape[0]
    tiles, tile = held.shape[:2]
    halo_fetch = pltpu.make_async_copy(halo_hbm, halo_ref, sems.at[tiles])
    weight_fetch = pltpu.make_async_copy(
        weight_hbm.at[pl.ds(width, width), :], weight_ref, sems.at[tiles + 1]
    )

    def push(number):
        return pltpu.make_async_copy(
            held.at[number], pre_grad_hbm.at[pl.ds(number * tile, tile), :], sems.at[number]
        )

    halo_fetch.start()
    weight_fetch.start()
    small[...] = jnp.zeros_like(small)
    for step in range(tiles):
        rows = slice(step * tile, (step + 1) * tile)

        def add(ref, place, value):
            if step == 0:
                ref[place] = value
            else:
                ref[place] += value

        receivers = pick_columns(rows_ref[1:2, rows], nodes)
        message_grad = ecot_ref[rows, :].astype(F32) + tn(receivers, agg_grad_ref[...])
        normed = norm_ref[rows, :].astype(F32)
        small[1:2] += jnp.sum(message_grad * normed, axis=0, keepdims=True)
        grad_norm = norm_backward(
            message_grad * gain_ref[...], normed, inv_ref[rows, :]
        ).astype(BF16)
        grad_pre = nt(grad_norm, weight_out_ref[...]) * slope_ref[rows, :].astype(F32)
        grad_pre = grad_pre.astype(BF16)
        held[step] = grad_pre
        push(step).start()
        small[0:1] += jnp.sum(grad_pre.astype(F32), axis=0, keepdims=True)
        add(grad_out, slice(None), tn(act_ref[rows, :], grad_norm))
        add(grad_in, slice(0, width), tn(edge_ref[rows, :], grad_pre))
        senders = pick_columns(rows_ref[0:1, rows], nodes + slots)
        add(sums, slice(0, nodes + slots), nn(senders, grad_pre))
        add(sums, slice(nodes + slots, None), nn(receivers, grad_pre))
    halo_fetch.wait()
    weight_fetch.wait()
    own = sums[:nodes].astype(BF16)
    remote = sums[nodes : nodes + slots].astype(BF16)
    received = sums[nodes + slots :].astype(BF16)
    sums_ref[:nodes] = own
    sums_ref[nodes:] = received
    terms_ref[...] = nt(remote, weight_ref[...]).astype(BF16)
    hidden = hidden_ref[...]
    grad_in[width : 2 * width] = tn(hidden, own) + tn(halo_ref[...], remote)
    grad_in[2 * width :] = tn(hidden, received)
    core = core_ref[0]
    for dst, side in ((send_ref, 1 - core), (keep_ref, core)):

        def pack(chip, carry):
            piece = chip * 2 + side
            row = pl.multiple_of(chip * EDGE_BLOCK, EDGE_BLOCK)
            start = pl.multiple_of(piece * EDGE_IN, EDGE_IN)
            dst[pl.ds(row, EDGE_IN), :] = grad_in[pl.ds(start, EDGE_IN), :].astype(BF16)
            row = pl.multiple_of(row + EDGE_IN, EDGE_OUT)
            start = pl.multiple_of(piece * EDGE_OUT, EDGE_OUT)
            dst[pl.ds(row, EDGE_OUT), :] = grad_out[pl.ds(start, EDGE_OUT), :].astype(BF16)
            return carry

        lax.fori_loop(0, 16, pack, 0, unroll=4)
        dst[16 * EDGE_BLOCK :, :] = small[...].astype(BF16)
    for number in range(tiles):
        push(number).wait()


def pair_kernel(
    batch_ref, keep_ref, recv_ref, nkeep_ref, nrecv_ref,
    mine_ref, one_ref, two_ref, three_ref, states
):
    def both(start, count):
        rows = slice(start, start + count)
        return keep_ref[rows, :].astype(F32) + recv_ref[rows, :].astype(F32)

    def node_both(start, count):
        rows = slice(start, start + count)
        return nkeep_ref[rows, :].astype(F32) + nrecv_ref[rows, :].astype(F32)

    for chip in range(16):
        start = chip * EDGE_BLOCK
        into, out = both(start, EDGE_IN), both(start + EDGE_IN, EDGE_OUT)
        row = chip * SHARE_EDGE
        for state in range(STATES):
            states[state, row : row + SHARE_EDGE_IN, :] = into[
                state * SHARE_EDGE_IN : (state + 1) * SHARE_EDGE_IN
            ]
            states[state, row + SHARE_EDGE_IN : row + SHARE_EDGE, :] = out[
                state * SHARE_EDGE_OUT : (state + 1) * SHARE_EDGE_OUT
            ]
    small = both(16 * EDGE_BLOCK, SMALL) + node_both(STATES * SHARE_NODE, SMALL)
    for state in range(STATES):
        states[state, 16 * SHARE_EDGE : SHARE_ROWS, :] = node_both(state * SHARE_NODE, SHARE_NODE)
        states[state, SHARE_ROWS:, :] = small
    for away, ref in enumerate((mine_ref, one_ref, two_ref, three_ref)):
        ref[...] = states[lax.rem(batch_ref[0] + away, STATES)].astype(BF16)


def merge_kernel(mine_ref, one_ref, two_ref, three_ref, out_ref, block):
    total = (
        mine_ref[...].astype(F32)
        + one_ref[...].astype(F32)
        + two_ref[...].astype(F32)
        + three_ref[...].astype(F32)
    )
    chips, _, width = block.shape
    block[:, :16, :] = total[:256].reshape(chips, 16, width)
    block[:, 16:24, :] = total[256:384].reshape(chips, 8, width)
    for chip in range(chips):
        block[chip, 24:28, :] = total[384 + chip * 4 : 388 + chip * 4]
        block[chip, 28:32, :] = total[SHARE_ROWS : SHARE_ROWS + 4]
    out_ref[...] = block[...].astype(BF16)


def edge_out_kernel(ecot_ref, pre_grad_ref, weight_ref, out_ref):
    out_ref[...] = (
        ecot_ref[...].astype(F32) + nt(pre_grad_ref[...], weight_ref[...])
    ).astype(BF16)


def nodes_kernel(
    halo_ref, rows_ref, sums_ref, weight_ref, grad_pre_ref, nweight_ref, cot_ref, out_ref
):
    nodes, width = cot_ref.shape
    picks = pick_columns(rows_ref[...], nodes)
    out_ref[...] = (
        cot_ref[...].astype(F32)
        + nt(grad_pre_ref[...], nweight_ref[...])
        + nt(sums_ref[:nodes], weight_ref[width : 2 * width])
        + nt(sums_ref[nodes:], weight_ref[2 * width :])
        + nn(picks, halo_ref[...])
    ).astype(BF16)


def finish_kernel(factor, arrived_ref, edge_in_ref, edge_out_ref, node_in_ref, node_out_ref, small_ref):
    total = jnp.sum(arrived_ref[...].astype(F32), axis=0) * factor
    row = 0
    for ref in (edge_in_ref, edge_out_ref, node_in_ref, node_out_ref, small_ref):
        count = ref.shape[0]
        ref[...] = total[row : row + count, :]
        row += count


def call(body, outs, grid=None, in_specs=None, out_specs=None, scratch=(), cost=None, limit=None):
    args = {}
    if grid is not None:
        args = dict(grid=grid, in_specs=in_specs, out_specs=out_specs)
    elif in_specs is not None:
        args = dict(in_specs=in_specs)
        if out_specs is not None:
            args["out_specs"] = tuple(out_specs)
    return pl.pallas_call(
        body,
        out_shape=outs,
        scratch_shapes=scratch,
        compiler_params=pltpu.CompilerParams(vmem_limit_bytes=limit or VMEM_MOST),
        cost_estimate=cost,
        **args,
    )


def flops(count, moved):
    return pl.CostEstimate(flops=int(count), bytes_accessed=int(moved), transcendentals=0)


def shape(*dims, dtype=BF16):
    return jax.ShapeDtypeStruct(dims, dtype)


def far(*dims, dtype=BF16):
    return pltpu.HBM(dims, dtype)


def keep_far(*arrays):
    return [pltpu.with_memory_space_constraint(item, pltpu.HBM) for item in arrays]


def full(*dims):
    return pl.BlockSpec(dims, lambda i: (0,) * len(dims))


def tiled(*dims):
    return pl.BlockSpec(dims, lambda i: (i,) + (0,) * (len(dims) - 1))


SCALAR = pl.BlockSpec(memory_space=pltpu.SMEM)
FAR = pl.BlockSpec(memory_space=pltpu.HBM)
WHOLE = pl.BlockSpec(memory_space=pltpu.VMEM)


def shards(
    node_latents, edge_latents, node_cotangent, edge_cotangent, senders, receivers, send_rows,
    edge_weight_in, edge_bias, edge_weight_out, edge_gain,
    node_weight_in, node_bias, node_weight_out, node_gain,
):
    nodes, width = node_latents.shape[1:]
    edges = edge_latents.shape[1]
    parts = lax.axis_size("nodes")
    batch_size = lax.axis_size("batch")
    slots = send_rows.shape[1] * send_rows.shape[2]
    hidden = node_latents[0]
    edge_rows = edge_latents[0]
    ncot = node_cotangent[0]
    ecot = edge_cotangent[0]
    node_index = lax.axis_index("nodes")
    core = jnp.reshape(node_index % 2, (1,)).astype(jnp.int32)
    batch = jnp.reshape(lax.axis_index("batch"), (1,)).astype(jnp.int32)
    tile = min(TILE, edges)
    grid = (edges // tile,)

    row = lambda vector: vector.reshape(1, width)
    index_rows = jnp.stack([senders, receivers], axis=0)

    partner = [(i, i ^ batch_size) for i in range(parts * batch_size)]
    places = [
        [(n * batch_size + b, n * batch_size + (b + away) % batch_size)
         for n in range(parts) for b in range(batch_size)]
        for away in (1, 2, 3)
    ]

    with jax.named_scope("halo_rows"):
        outgoing = call(gather_kernel, shape(slots, width), limit=VMEM_FEW)(
            *keep_far(send_rows[0].T, hidden)
        )
        halo = lax.all_to_all(
            outgoing.reshape(parts, -1, width), "nodes", 0, 0, tiled=True
        ).reshape(slots, width)
    rows_tile = pl.BlockSpec((2, tile), lambda i: (0, i))
    edge_tile = tiled(tile, width)
    node_full = full(nodes, width)
    node_f32 = shape(nodes, width, dtype=F32)
    with jax.named_scope("edge_pre_local"):
        part, npart, ordered = call(
            local_kernel,
            (far(edges, width, dtype=F32), far(nodes, width, dtype=F32), far(nodes, width)),
            grid,
            [
                edge_tile, rows_tile, node_full, full(3 * width, width), full(1, width),
                full(width, width), full(1, width),
            ],
            (edge_tile, node_full, node_full),
            [pltpu.VMEM((2 * nodes, width), BF16)],
            flops(2 * edges * width * 2 * width, 6 * edges * width),
        )(edge_rows, index_rows, hidden, edge_weight_in, row(edge_bias), node_weight_in, row(node_bias))
    with jax.named_scope("forward"):
        node_pair = shape(STATES * SHARE_NODE + SMALL, width)
        act, slope, norm, inv, node_grad_pre, agg_grad, nsend, nkeep = call(
            forward_kernel,
            (
                shape(edges, width), shape(edges, width), shape(edges, width),
                shape(edges, 1, dtype=F32), far(nodes, width), shape(nodes, width),
                node_pair, far(*node_pair.shape),
            ),
            None,
            [SCALAR, WHOLE, WHOLE, WHOLE] + [FAR] * 9,
            None,
            [
                pltpu.VMEM((slots, width), BF16), pltpu.VMEM((nodes, width), F32),
                pltpu.VMEM((3, STATES, 2, 64, width), F32), pltpu.VMEM((SMALL, width), F32),
                pltpu.VMEM((edges // tile, tile, width), F32), pltpu.VMEM((slots, width), BF16),
                pltpu.VMEM((width, width), BF16), pltpu.VMEM((width, width), BF16),
                pltpu.VMEM((nodes, width), BF16), pltpu.VMEM((nodes, width), F32),
                pltpu.VMEM((2 * width, width), BF16), pltpu.VMEM((width, width), BF16),
                pltpu.VMEM((nodes, width), BF16), pltpu.SemaphoreType.DMA((edges // tile + 8,)),
            ],
            flops(2 * edges * width * 3 * width, 12 * edges * width),
            VMEM_FEW,
        )(
            core, index_rows, row(edge_gain), row(node_gain),
            *keep_far(
                part, halo, edge_weight_in, edge_weight_out, ordered, npart, node_weight_in,
                node_weight_out, ncot,
            ),
        )
    with jax.named_scope("node_weight_pair"):
        nrecv = lax.ppermute(nsend, ALL, partner)
    with jax.named_scope("backward"):
        edge_pair = shape(16 * EDGE_BLOCK + SMALL, width)
        pre_grad, esend, ekeep, sums, terms = call(
            backward_kernel,
            (
                far(edges, width), edge_pair, far(*edge_pair.shape), far(2 * nodes, width),
                far(slots, width),
            ),
            None,
            [SCALAR] + [WHOLE] * 11 + [FAR, FAR],
            [FAR] + [WHOLE] * 4,
            [
                pltpu.VMEM((3 * width, width), F32), pltpu.VMEM((width, width), F32),
                pltpu.VMEM((2 * nodes + slots, width), F32), pltpu.VMEM((SMALL, width), F32),
                pltpu.VMEM((slots, width), BF16), pltpu.VMEM((width, width), BF16),
                pltpu.VMEM((edges // tile, tile, width), BF16),
                pltpu.SemaphoreType.DMA((edges // tile + 2,)),
            ],
            flops(2 * edges * width * 6 * width, 14 * edges * width),
            VMEM_FEW,
        )(
            core, ecot, index_rows, act, slope, norm, inv, edge_rows, agg_grad,
            row(edge_gain), edge_weight_out, hidden, *keep_far(halo, edge_weight_in),
        )
    with jax.named_scope("edge_weight_pair"):
        erecv = lax.ppermute(esend, ALL, partner)
    with jax.named_scope("halo_back"):
        back = lax.all_to_all(
            terms.reshape(parts, -1, width), "nodes", 0, 0, tiled=True
        ).reshape(slots, width)
    with jax.named_scope("pair_sum"):
        block = shape(SHARE_ROWS + SMALL, width)
        blocks = call(
            pair_kernel, (block,) * STATES, in_specs=[SCALAR] + [WHOLE] * 4,
            scratch=[pltpu.VMEM((STATES, *block.shape), F32)],
            cost=flops(0, 8 * edges * width), limit=VMEM_FEW,
        )(batch, *keep_far(ekeep), erecv, *keep_far(nkeep), nrecv)
    with jax.named_scope("weight_states"):
        got = [lax.ppermute(item, ALL, perm) for item, perm in zip(blocks[1:], places)]
    with jax.named_scope("grad_edges"):
        grad_edges = call(
            edge_out_kernel,
            shape(edges, width),
            grid,
            [edge_tile, edge_tile, full(width, width)],
            edge_tile,
            cost=flops(2 * edges * width * width, 6 * edges * width), limit=VMEM_FEW,
        )(*keep_far(ecot, pre_grad, edge_weight_in))
    with jax.named_scope("merge"):
        got, grad_edges = lax.optimization_barrier((got, grad_edges))
        sent = call(
            merge_kernel, shape(16, 32, width),
            scratch=[pltpu.VMEM((16, 32, width), F32)], limit=VMEM_FEW,
        )(blocks[0], *got)
    with jax.named_scope("chip_exchange"):
        chips = parts // 2
        groups = [[2 * chip + side for chip in range(chips)] for side in range(2)]
        arrived = lax.all_to_all(sent, "nodes", 0, 0, tiled=True, axis_index_groups=groups)
    with jax.named_scope("grad_nodes"):
        near_weight = pl.BlockSpec((width, width), lambda i: (0, 0))
        grad_nodes = call(
            nodes_kernel, shape(nodes, width), (1,),
            [
                full(slots, width), full(1, slots), full(2 * nodes, width), full(3 * width, width),
                full(nodes, width), near_weight, full(nodes, width),
            ],
            full(nodes, width), limit=VMEM_FEW,
        )(
            back, send_rows.reshape(1, slots),
            *keep_far(sums, edge_weight_in, node_grad_pre, node_weight_in, ncot),
        )
    with jax.named_scope("weight_grads"):
        factor = 1.0 / math.sqrt(batch_size * edges * parts)
        edge_in, edge_out, node_in, node_out, small = call(
            functools.partial(finish_kernel, factor),
            (
                shape(12, width, dtype=F32), shape(4, width, dtype=F32), shape(8, width, dtype=F32),
                shape(4, width, dtype=F32), shape(4, width, dtype=F32),
            ),
            limit=VMEM_FEW,
        )(arrived)
        place = node_index * batch_size + lax.axis_index("batch")
        small = lax.dynamic_slice(small, (0, place * 4), (4, 4))
    return (
        grad_nodes[None], grad_edges[None], edge_in, small[0], edge_out, small[1],
        node_in, small[2], node_out, small[3],
    )


def solution(mesh):
    rows = P("batch", "nodes", None)
    split = P(ALL, None)
    return jax.shard_map(
        shards,
        mesh=mesh,
        in_specs=(rows,) * 4 + (P("nodes"), P("nodes"), P("nodes", None, None)) + (P(),) * 8,
        out_specs=(rows, rows) + (split, P(ALL)) * 4,
        check_vma=False,
    )
```
